128 devices in a mesh: face: 4 (over z_hi, core), tile: 32 (over y, z_lo, x).
Axes of the slice: x: 4, y: 4, z: 4 (z_hi: 2, z_lo: 2; z = z_hi * 2 + z_lo), core: 2. Of those that a mesh axis runs over, the one named last changes fastest.
Arguments:
- state: float32 [4, 16, 3072, 768], P(None, None, ('face', 'tile')), may hold values from -6 to 6
- wave_speed: float32 [16], replicated, may hold values from 0.1 to 0.45
- seam_turns: int32 [4], replicated, may hold values from 0 to 3
- layer_mass: float32 [16], replicated, may hold values from 0.5 to 2
- link_source: int32 [128, 128, 128], P(('face', 'tile')), may hold values from 0 to 18431
- link_row: int32 [128, 128, 128], P(('face', 'tile')), may hold values from 0 to 3, as said below
- link_weight: float32 [128, 128, 128], P(('face', 'tile')), may hold values from 0.1 to 1
- link_count: int32 [128, 128], P(('face', 'tile')), may hold values from 42 to 128, as said below
Outputs:
- new_state: float32 [4, 16, 3072, 768], P(None, None, ('face', 'tile'))
- zonal_means: float32 [512, 64], P(('face', 'tile'))
- streamfunction: float32 [512, 16], P(('face', 'tile'))
The draws below stay inside these ranges and needn't reach their ends.
Inputs may be any that keep to these rules, and one draw needn't show every extreme that they name: `link_row`: slot j below 4 of every tile and band holds row j. `link_count`: every tile has a full count 128 to some band and every band receives a full count from some tile.
All inputs are finite; a program needn't handle non-finite values.
Results may differ from the reference program's by a relative error of at most 0.0003.
Values sent between devices are 32-bit elements; how exact they have to be, the bound alone decides.
A program may use at most 128 MiB of HBM per device.

```python
import math
import jax
import jax.numpy as jnp
from jax import lax

FACE_N = 768
COLS_DEV = 24
LEVELS = 16
SUBSTEPS = 4
BAND_ROWS = 4
SLOTS = 128
NX = 3072
LAT = 512
N_FACE = 4
N_TILE = 32


def draw_link_source(key, part):
    key = jax.random.fold_in(key, 11)
    devices = N_FACE * N_TILE
    key_x, key_y = jax.random.split(key)
    shape = (devices, devices, SLOTS)
    base = (jnp.arange(devices, dtype=jnp.int32) * FACE_N // devices)[None, :, None]
    span = FACE_N // devices + 2
    merid = jnp.minimum(base + jax.random.randint(key_y, shape, 0, span), FACE_N - 1)
    zonal = jax.random.randint(key_x, shape, 0, COLS_DEV)
    return (zonal * FACE_N + merid).astype(jnp.int32)


def draw_link_row(key, part):
    key = jax.random.fold_in(key, 12)
    devices = N_FACE * N_TILE
    rows = jax.random.randint(key, (devices, devices, SLOTS), 0, BAND_ROWS)
    slot = jnp.arange(SLOTS, dtype=jnp.int32)[None, None, :]
    return jnp.where(slot < BAND_ROWS, slot, rows).astype(jnp.int32)


def draw_link_count(key, part):
    key = jax.random.fold_in(key, 13)
    devices = N_FACE * N_TILE
    key_c, key_p = jax.random.split(key)
    counts = jax.random.randint(key_c, (devices, devices), SLOTS // 3, SLOTS + 1)
    order = jax.random.permutation(key_p, devices)
    counts = counts.at[jnp.arange(devices), order].set(SLOTS)
    return counts.astype(jnp.int32)


def touch_ends(drawn, own_key, low, high):
    shape = drawn.shape
    place = [jax.random.randint(jax.random.fold_in(own_key, axis), (), 0, shape[axis]) for axis in range(len(shape))]
    drawn = drawn.at[tuple(place)].set(low)
    longest = shape.index(max(shape))
    place[longest] = (place[longest] + 1) % shape[longest]
    return drawn.at[tuple(place)].set(high)


def block_scale(stream_key, shape, shards, low, largest):
    gain, own = 1.0, jax.random.fold_in(stream_key, 6)
    for axis_at, blocks in shards:
        draws = jnp.exp(jax.random.uniform(jax.random.fold_in(own, axis_at), (blocks,), jnp.float32, low / len(shards), largest / len(shards)))
        gain = gain * jnp.repeat(draws, shape[axis_at] // blocks).reshape([-1 if axis == axis_at else 1 for axis in range(len(shape))])
    return gain


def centred(key, dims, deviation, limit, cuts=(), kind=jnp.bfloat16):
    values = jax.random.normal(key, dims, jnp.float32) * deviation
    if len(cuts) > 0:
        values = block_scale(key, dims, cuts, -0.22, 0.18) * values
    return jnp.clip(values, min=-limit, max=limit).astype(kind)


def setup_inputs(seed: int = 0) -> dict:
    seeds = jax.random.split(jax.random.key(seed), 9)
    state = centred(seeds[0], (4, LEVELS, NX, FACE_N), 1.0, 6.0, ((2, 128),), jnp.float32)
    wave_speed = jnp.clip(jnp.exp(jax.random.uniform(seeds[1], (LEVELS,), jnp.float32, math.log(0.1), math.log(0.45))), 0.1, 0.45)
    seam_turns = touch_ends(jax.random.randint(seeds[2], (N_FACE,), 0, 4), jax.random.fold_in(seeds[2], 1), 0, 3).astype(jnp.int32)
    layer_mass = jnp.clip(jnp.exp(jax.random.uniform(seeds[3], (LEVELS,), jnp.float32, math.log(0.5), math.log(2.0))), 0.5, 2.0)
    link_source = draw_link_source(jax.random.fold_in(seeds[8], 71), 0)
    link_row = draw_link_row(jax.random.fold_in(seeds[8], 71), 0)
    link_weight = jnp.clip(jnp.exp(math.log(1.0) - 2.3025851 * jax.random.uniform(seeds[6], (N_FACE * N_TILE, N_FACE * N_TILE, SLOTS), jnp.float32) ** block_scale(seeds[6], (N_FACE * N_TILE, N_FACE * N_TILE, SLOTS), ((0, 128),), -0.2, 0.2)), 0.1, 1.0)
    link_count = draw_link_count(jax.random.fold_in(seeds[8], 71), 0)
    return dict(state=state, wave_speed=wave_speed, seam_turns=seam_turns, layer_mass=layer_mass, link_source=link_source, link_row=link_row, link_weight=link_weight, link_count=link_count)


viscosity = 0.1


def turn_parts(code):
    cosine = jnp.where(code == 0, 1.0, jnp.where(code == 2, -1.0, 0.0)).astype(jnp.float32)
    sine = jnp.where(code == 1, 1.0, jnp.where(code == 3, -1.0, 0.0)).astype(jnp.float32)
    return cosine, sine


def neighbours_y(field):
    upper = jnp.pad(field[..., 1:], ((0, 0), (0, 0), (0, 1)))
    lower = jnp.pad(field[..., :-1], ((0, 0), (0, 0), (1, 0)))
    return upper, lower


def update(centre, left, right, courant):
    slopes_x = []
    slopes_y = []
    laps = []
    for index in range(4):
        upper, lower = neighbours_y(centre[index])
        slopes_x.append(0.5 * (right[index] - left[index]))
        slopes_y.append(0.5 * (upper - lower))
        laps.append(left[index] + right[index] + upper + lower - 4.0 * centre[index])
    divergence = slopes_x[0] + slopes_y[1]
    east = centre[0] - courant * (slopes_x[3] + 0.5 * slopes_x[2]) + viscosity * laps[0]
    north = centre[1] - courant * (slopes_y[3] + 0.5 * slopes_y[2]) + viscosity * laps[1]
    heat = centre[2] - 0.5 * courant * divergence + viscosity * laps[2]
    thick = centre[3] - courant * divergence + viscosity * laps[3]
    return jnp.stack([east, north, heat, thick])


def substep(state, courant, seam_turns):
    width = COLS_DEV * N_TILE
    positions = jnp.arange(NX, dtype=jnp.int32)
    face_of = positions // width
    left_cos, left_sin = turn_parts(seam_turns[face_of])
    right_cos, right_sin = turn_parts(seam_turns[(face_of + 1) % N_FACE])
    right_sin = -right_sin
    at_left = (positions % width == 0)[None, :, None]
    at_right = (positions % width == width - 1)[None, :, None]
    left = [jnp.roll(state[index], 1, axis=1) for index in range(4)]
    right = [jnp.roll(state[index], -1, axis=1) for index in range(4)]
    lc = left_cos[None, :, None]
    lsn = left_sin[None, :, None]
    rc = right_cos[None, :, None]
    rsn = right_sin[None, :, None]
    turned_east = lc * left[0] - lsn * left[1]
    turned_north = lsn * left[0] + lc * left[1]
    left[0] = jnp.where(at_left, turned_east, left[0])
    left[1] = jnp.where(at_left, turned_north, left[1])
    turned_east = rc * right[0] - rsn * right[1]
    turned_north = rsn * right[0] + rc * right[1]
    right[0] = jnp.where(at_right, turned_east, right[0])
    right[1] = jnp.where(at_right, turned_north, right[1])
    return update(state, left, right, courant)


def reference(state, wave_speed, seam_turns, layer_mass, link_source, link_row, link_weight, link_count):
    courant = wave_speed[:, None, None]
    fields = state
    for step in range(SUBSTEPS):
        fields = substep(fields, courant, seam_turns)
    devices = N_FACE * N_TILE
    channel_count = 5 * LEVELS

    def one_tile(carry, tile):
        sums, weights = carry
        slab = lax.dynamic_slice_in_dim(fields, tile * COLS_DEV, COLS_DEV, 2)
        flux = slab[1] * (layer_mass[:, None, None] + slab[3])
        channels = jnp.concatenate([slab.reshape(4 * LEVELS, -1), flux.reshape(LEVELS, -1)], axis=0)
        cells = link_source[tile].reshape(-1)
        gathered = jnp.take(channels, cells, axis=1)
        live = jnp.arange(SLOTS, dtype=jnp.int32)[None, :] < link_count[tile][:, None]
        live_weight = jnp.where(live, link_weight[tile], 0.0).reshape(-1)
        global_row = (jnp.arange(devices, dtype=jnp.int32)[:, None] * BAND_ROWS + link_row[tile]).reshape(-1)
        sums = sums + jax.ops.segment_sum((gathered * live_weight[None, :]).T, global_row, LAT)
        weights = weights + jax.ops.segment_sum(live_weight, global_row, LAT)
        return (sums, weights), None

    start = (jnp.zeros((LAT, channel_count), jnp.float32), jnp.zeros((LAT,), jnp.float32))
    (sums, weights), unused = lax.scan(one_tile, start, jnp.arange(devices, dtype=jnp.int32))
    means = sums / weights[:, None]
    zonal = means[:, :4 * LEVELS]
    flux_mean = means[:, 4 * LEVELS:]
    latitude = ((jnp.arange(LAT, dtype=jnp.float32) + 0.5) / LAT - 0.5) * (jnp.pi / 2)
    stream = jnp.cos(latitude)[:, None] * jnp.cumsum(flux_mean, axis=1)
    return fields, zonal, stream
```

```python
import jax
import jax.numpy as jnp
from jax import lax
from jax.experimental import pallas as pl
from jax.experimental.pallas import tpu as pltpu
from jax.sharding import PartitionSpec as P

SUBSTEPS = 4
BAND_ROWS = 4
FIELDS = 4
GROUP = 8
LANES = 128
GATHERED = 8
SCALE = 10.0**-SUBSTEPS

f32 = jnp.float32
bf16 = jnp.bfloat16


def north_of(q):
    width = q.shape[1]
    rolled = pltpu.roll(q, width - 1, 1)
    tail = rolled[:, width - LANES :]
    lane = lax.broadcasted_iota(jnp.int32, tail.shape, 1)
    tail = jnp.where(lane == LANES - 1, 0.0, tail)
    return jnp.concatenate([rolled[:, : width - LANES], tail], axis=1)


def south_of(q):
    rolled = pltpu.roll(q, 1, 1)
    head = rolled[:, :LANES]
    lane = lax.broadcasted_iota(jnp.int32, head.shape, 1)
    head = jnp.where(lane == 0, 0.0, head)
    return jnp.concatenate([head, rolled[:, LANES:]], axis=1)


def turned(wind, turn):
    cosine, sine = turn
    east, north = wind
    return cosine * east - sine * north, sine * east + cosine * north


def column(source, target, group, at, courant, turn_west=None, turn_east=None):
    mid = [source[group, at, c] for c in range(FIELDS)]
    west = [source[group, at - 1, c] for c in range(FIELDS)]
    east = [source[group, at + 1, c] for c in range(FIELDS)]
    if turn_west is not None:
        west[0], west[1] = turned(west[:2], turn_west)
    if turn_east is not None:
        east[0], east[1] = turned(east[:2], turn_east)
    north = [north_of(q) for q in mid]
    south = [south_of(q) for q in mid]
    base = [
        6.0 * mid[c] + ((west[c] + east[c]) + (north[c] + south[c]))
        for c in range(FIELDS)
    ]
    spread = courant * ((east[0] - west[0]) + (north[1] - south[1]))
    push_x = courant * ((east[3] - west[3]) + (east[2] - west[2]))
    push_y = courant * ((north[3] - south[3]) + (north[2] - south[2]))
    target[group, at, 0] = base[0] - push_x
    target[group, at, 1] = base[1] - push_y
    target[group, at, 2] = base[2] - 0.25 * spread
    target[group, at, 3] = base[3] - spread


def quarter(code):
    cosine = jnp.where(code == 0, 1.0, jnp.where(code == 2, -1.0, 0.0))
    sine = jnp.where(code == 1, 1.0, jnp.where(code == 3, -1.0, 0.0))
    return cosine.astype(f32), sine.astype(f32)


def per_level(scalars, group):
    level = lax.broadcasted_iota(jnp.int32, (GROUP, LANES), 0)
    out = jnp.zeros((GROUP, LANES), f32)
    for k in range(GROUP):
        out = jnp.where(level == k, scalars[group * GROUP + k], out)
    return out


def split(value):
    high = value.astype(bf16)
    return high, (value - high.astype(f32)).astype(bf16)


def kernel(
    n_face, n_tile, cols, halo,
    wave, turns, mass, counts, state, source, row, weight,
    new_state, zonal, stream,
    first, odd, even, slab, cells, picked, courants, masses, rows, weights,
    spots0, spots1, sums, inbox,
    load_sem, row_sem, weight_sem, store_sem, spot_sem, send_sem, recv_sem,
    out_sem, in_sem,
):
    face, tile = lax.axis_index("face"), lax.axis_index("tile")
    devices = n_face * n_tile
    me = face * n_tile + tile
    levels = wave.shape[0]
    groups = levels // GROUP
    width = state.shape[2]
    repeat = width // LANES
    mesh_id = pl.DeviceIdType.MESH

    def place(index):
        index = lax.rem(index, devices)
        return lax.div(index, n_tile), lax.rem(index, n_tile)

    right, left = place(me + 1), place(me + devices - 1)

    def strip(ref, j):
        return ref.at[:, :, pl.ds(j * LANES, LANES)]

    loads = [
        pltpu.make_async_copy(strip(state, j), slab.at[:, j], load_sem.at[j])
        for j in range(repeat)
    ]
    for load in loads:
        load.start()
    row_load = pltpu.make_async_copy(row, rows, row_sem)
    row_load.start()
    weight_load = pltpu.make_async_copy(weight, weights, weight_sem)
    weight_load.start()

    barrier = pltpu.get_barrier_semaphore()

    def greet(i, carry):
        pl.semaphore_signal(barrier, inc=1, device_id=place(me + i), device_id_type=mesh_id)
        return carry

    lax.fori_loop(1, devices, greet, 0)

    for g in range(groups):
        courants[g] = 5.0 * per_level(wave, g)
        masses[g] = per_level(mass, g)

    def wide(value):
        return jnp.concatenate([value] * repeat, axis=1)

    def lift(g, x):
        for c in range(FIELDS):
            for j in range(repeat):
                lifted = slab[c, j, pl.ds(g * GROUP * cols + x, GROUP, stride=cols), :]
                lifted = 0.5 * lifted if c == 2 else lifted
                first[g, x + halo, c, :, pl.ds(j * LANES, LANES)] = lifted

    for load in loads:
        load.wait()

    def lift_edge(i, carry):
        g, j = lax.div(i, 2 * halo), lax.rem(i, 2 * halo)
        lift(g, j + (cols - 2 * halo) * lax.div(j, halo))
        return carry

    lax.fori_loop(0, groups * 2 * halo, lift_edge, 0)

    pl.semaphore_wait(barrier, devices - 1)

    def halo_copy(side, g):
        if side == 0:
            here, there, to = cols, 0, right
        else:
            here, there, to = halo, cols + halo, left
        return pltpu.make_async_remote_copy(
            src_ref=first.at[g, pl.ds(here, halo)],
            dst_ref=first.at[g, pl.ds(there, halo)],
            send_sem=send_sem.at[side, g],
            recv_sem=recv_sem.at[side, g],
            device_id=to,
            device_id_type=mesh_id,
        )

    for g in range(groups):
        for side in range(2):
            halo_copy(side, g).start()

    def lift_inner(i, carry):
        n = cols - 2 * halo
        lift(lax.div(i, n), halo + lax.rem(i, n))
        return carry

    lax.fori_loop(0, groups * (cols - 2 * halo), lift_inner, 0)

    steps = [(first, odd), (odd, even), (even, odd), (odd, even)]

    for s, (old, new) in enumerate(steps, 1):
        n = cols - 2 * s

        def inner(i, carry, old=old, new=new, s=s, n=n):
            g, x = lax.div(i, n), lax.rem(i, n)
            column(old, new, g, x + s + halo, wide(courants[g]))
            return carry

        lax.fori_loop(0, groups * n, inner, 0, unroll=2)

    lane = lax.broadcasted_iota(jnp.int32, (GROUP, width), 1)

    def finish(x):
        values = {}
        for g in range(groups):
            for c in range(FIELDS):
                value = even[g, x + halo, c] * (2.0 * SCALE if c == 2 else SCALE)
                for j in range(repeat):
                    part = value[:, j * LANES : (j + 1) * LANES]
                    slab[c, j, pl.ds(g * GROUP * cols + x, GROUP, stride=cols), :] = part
                values[c, g] = value
        blocks = [values[c, g] for c in range(FIELDS) for g in range(groups)]
        blocks += [values[1, g] * (wide(masses[g]) + values[3, g]) for g in range(groups)]
        blocks.append(jnp.ones((GROUP, width), f32))
        spare = LANES - GROUP * len(blocks)
        blocks.append(jnp.zeros((spare, width), f32))
        start = pl.multiple_of(x * width, width)
        cells[pl.ds(start, width), :] = jnp.concatenate(blocks, axis=0).T

    def finish_inner(i, carry):
        finish(halo + i)
        return carry

    lax.fori_loop(0, cols - 2 * halo, finish_inner, 0)

    west_cos, west_sin = quarter(jnp.where(tile == 0, turns[face], 0))
    east_cos, east_sin = quarter(jnp.where(tile == n_tile - 1, turns[lax.rem(face + 1, n_face)], 0))

    def edges(g, carry):
        courant = wide(courants[g])
        halo_copy(0, g).wait_recv()
        for s, (old, new) in enumerate(steps, 1):
            for x in range(s - halo, s):
                column(
                    old, new, g, x + halo, courant,
                    turn_west=(west_cos, west_sin) if x == 0 else None,
                    turn_east=(west_cos, -west_sin) if x == -1 else None,
                )
        halo_copy(1, g).wait_recv()
        for s, (old, new) in enumerate(steps, 1):
            for x in range(cols - s, cols + halo - s):
                column(
                    old, new, g, x + halo, courant,
                    turn_west=(east_cos, east_sin) if x == cols else None,
                    turn_east=(east_cos, -east_sin) if x == cols - 1 else None,
                )
        return carry

    for g in range(groups):
        edges(g, 0)

    def finish_edge(i, carry):
        finish(i + (cols - 2 * halo) * lax.div(i, halo))
        return carry

    lax.fori_loop(0, 2 * halo, finish_edge, 0)

    stores = [
        pltpu.make_async_copy(slab.at[:, j], strip(new_state, j), store_sem.at[j])
        for j in range(repeat)
    ]
    for store in stores:
        store.start()

    row_load.wait()
    weight_load.wait()
    spots = (spots0, spots1)
    rounds = devices // GATHERED
    slots = rows.shape[1]

    def first_band(turn):
        return pl.multiple_of(lax.rem(lax.div(me, GATHERED) + turn, rounds) * GATHERED, GATHERED)

    def spot_copy(turn, slot):
        return pltpu.make_async_copy(
            source.at[pl.ds(first_band(turn), GATHERED)], spots[slot], spot_sem.at[slot]
        )

    def pick(slot):
        for k in range(GATHERED):
            for j in range(slots):
                picked[slot, k, pl.ds(j, 1), :] = cells[pl.ds(spots[slot][k, j], 1), :]

    sub = lax.broadcasted_iota(jnp.int32, (2 * BAND_ROWS, slots), 0)
    link = lax.broadcasted_iota(jnp.int32, (2 * BAND_ROWS, slots), 1)

    def add_up(turn, slot):
        start = first_band(turn)
        for k in range(GATHERED):
            band = start + k
            w = weights[pl.ds(band, 1), :]
            high = w.astype(bf16).astype(f32)
            part = jnp.where(sub < BAND_ROWS, high, w - high)
            mine = (rows[pl.ds(band, 1), :] == lax.rem(sub, BAND_ROWS)) & (link < counts[band])
            lhs = jnp.where(mine, part, 0.0).astype(bf16)
            high_cells, low_cells = split(picked[slot, k])
            product = jnp.dot(
                lhs,
                jnp.concatenate([high_cells, low_cells], axis=1),
                preferred_element_type=f32,
            )
            sums[band] = (
                product[:BAND_ROWS, :LANES]
                + product[:BAND_ROWS, LANES:]
                + product[BAND_ROWS:, :LANES]
            )
        for k in range(GATHERED):
            band = start + k

            @pl.when(band != me)
            def _():
                pltpu.make_async_remote_copy(
                    src_ref=sums.at[band],
                    dst_ref=inbox.at[me],
                    send_sem=out_sem,
                    recv_sem=in_sem,
                    device_id=place(band),
                    device_id_type=mesh_id,
                ).start()

            @pl.when(band == me)
            def _():
                inbox[me] = sums[band]

    spot_copy(0, 0).start()
    spot_copy(1, 1).start()

    def two_rounds(i, carry):
        for slot in range(2):
            turn = 2 * i + slot
            spot_copy(turn, slot).wait()
            pick(slot)

            @pl.when(turn + 2 < rounds)
            def _():
                spot_copy(turn + 2, slot).start()

            add_up(turn, slot)
        return carry

    lax.fori_loop(0, rounds // 2, two_rounds, 0)

    others = pltpu.make_async_remote_copy(
        src_ref=sums.at[pl.ds(0, devices - 1)],
        dst_ref=inbox.at[pl.ds(0, devices - 1)],
        send_sem=out_sem,
        recv_sem=in_sem,
        device_id=right,
        device_id_type=mesh_id,
    )
    others.wait_recv()
    total = jnp.sum(inbox[...], axis=0)
    ones_at = (FIELDS + 1) * levels
    means = total / jnp.broadcast_to(total[:, ones_at : ones_at + 1], total.shape)
    zonal[...] = means[:, : FIELDS * levels]
    lane = lax.broadcasted_iota(jnp.int32, means.shape, 1)
    k = 1
    while k < levels:
        means = means + jnp.where(lane >= FIELDS * levels + k, pltpu.roll(means, k, 1), 0.0)
        k *= 2
    lat_row = me * BAND_ROWS + lax.broadcasted_iota(jnp.int32, means.shape, 0)
    total_rows = BAND_ROWS * devices
    phi = ((lat_row.astype(f32) + 0.5) / total_rows - 0.5) * (jnp.pi / 2)
    means = jnp.cos(phi) * means
    stream[...] = means[:, FIELDS * levels : ones_at]

    for g in range(groups):
        for side in range(2):
            halo_copy(side, g).wait_send()
    others.wait_send()
    for store in stores:
        store.wait()


def on_device(n_face, n_tile, state, wave, turns, mass, source, row, weight, count):
    fields, levels, cols, width = state.shape
    halo = SUBSTEPS
    groups = levels // GROUP
    devices = n_face * n_tile
    slots = source.shape[2]
    merged = (fields, levels * cols, width)
    smem = pl.BlockSpec(memory_space=pltpu.SMEM)
    vmem = pl.BlockSpec(memory_space=pltpu.VMEM)
    hbm = pl.BlockSpec(memory_space=pl.ANY)
    field = pltpu.VMEM((groups, cols + 2 * halo, fields, GROUP, width), f32)
    dma = pltpu.SemaphoreType.DMA

    def body(*refs):
        kernel(n_face, n_tile, cols, halo, *refs)

    new_state, zonal, stream = pl.pallas_call(
        body,
        out_shape=(
            jax.ShapeDtypeStruct(merged, f32),
            jax.ShapeDtypeStruct((BAND_ROWS, fields * levels), f32),
            jax.ShapeDtypeStruct((BAND_ROWS, levels), f32),
        ),
        in_specs=[smem, smem, smem, smem, hbm, hbm, hbm, hbm],
        out_specs=(hbm, vmem, vmem),
        scratch_shapes=[
            field,
            field,
            field,
            pltpu.VMEM((fields, width // LANES, levels * cols, LANES), f32),
            pltpu.VMEM((cols * width, LANES), f32),
            pltpu.VMEM((2, GATHERED, slots, LANES), f32),
            pltpu.VMEM((groups, GROUP, LANES), f32),
            pltpu.VMEM((groups, GROUP, LANES), f32),
            pltpu.VMEM((devices, slots), jnp.int32),
            pltpu.VMEM((devices, slots), f32),
            pltpu.SMEM((GATHERED, slots), jnp.int32),
            pltpu.SMEM((GATHERED, slots), jnp.int32),
            pltpu.VMEM((devices, BAND_ROWS, LANES), f32),
            pltpu.VMEM((devices, BAND_ROWS, LANES), f32),
            dma((width // LANES,)),
            dma,
            dma,
            dma((width // LANES,)),
            dma((2,)),
            dma((2, groups)),
            dma((2, groups)),
            dma,
            dma,
        ],
        compiler_params=pltpu.CompilerParams(
            collective_id=1, has_side_effects=True, vmem_limit_bytes=56 * 2**20
        ),
    )(
        wave,
        turns,
        mass,
        count[0],
        state.reshape(merged),
        source[0],
        row[0],
        weight[0],
    )
    return new_state.reshape(state.shape), zonal, stream


def solution(mesh):
    n_face, n_tile = mesh.shape["face"], mesh.shape["tile"]
    both = ("face", "tile")
    zonal_dim = P(None, None, both, None)
    links = P(both, None, None)

    def program(*args):
        return on_device(n_face, n_tile, *args)

    return jax.shard_map(
        program,
        mesh=mesh,
        in_specs=(zonal_dim, P(), P(), P(), links, links, links, P(both, None)),
        out_specs=(zonal_dim, P(both, None), P(both, None)),
        check_vma=False,
    )
```

```python
import jax
import jax.numpy as jnp
from jax import lax
from jax.experimental import pallas as pl
from jax.experimental.pallas import tpu as pltpu
from jax.sharding import PartitionSpec as P

SUBSTEPS = 4
BAND_ROWS = 4
FIELDS = 4
GROUP = 8
LANES = 128
GATHERED = 8
HANDED = 16
SCALE = 10.0**-SUBSTEPS

f32 = jnp.float32
bf16 = jnp.bfloat16


def turned(wind, turn):
    cosine, sine = turn
    east, north = wind
    return cosine * east - sine * north, sine * east + cosine * north


def strip(source, target, group, at, count, courant, turns=None):
    turns = turns or {}
    blocks = source.shape[4] // LANES
    lane = lax.broadcasted_iota(jnp.int32, (GROUP, LANES), 1)
    first_lane, last_lane = lane == 0, lane == LANES - 1
    inside = range(count)

    def mids(j):
        return {
            (k, c): source[group, at + k, c, :, pl.ds(j * LANES, LANES)]
            for k in inside
            for c in range(FIELDS)
        }

    def rolls(mid, amount):
        return {key: pltpu.roll(q, amount, 1) for key, q in mid.items()}

    mid = mids(0)
    up, down = rolls(mid, LANES - 1), rolls(mid, 1)
    zeros = {key: jnp.zeros((GROUP, LANES), f32) for key in mid}
    down_before = zeros
    for j in range(blocks):
        if j + 1 < blocks:
            mid_next = mids(j + 1)
            up_next, down_next = rolls(mid_next, LANES - 1), rolls(mid_next, 1)
        else:
            mid_next, up_next, down_next = None, zeros, None
        here = dict(mid)
        for k in (-1, count):
            for c in range(FIELDS):
                here[k, c] = source[group, at + k, c, :, pl.ds(j * LANES, LANES)]
        for k in inside:
            west = [here[k - 1, c] for c in range(FIELDS)]
            east = [here[k + 1, c] for c in range(FIELDS)]
            if k - 1 in turns:
                west[:2] = turned(west[:2], turns[k - 1])
            if k in turns:
                cosine, sine = turns[k]
                east[:2] = turned(east[:2], (cosine, -sine))
            north = [jnp.where(last_lane, up_next[k, c], up[k, c]) for c in range(FIELDS)]
            south = [jnp.where(first_lane, down_before[k, c], down[k, c]) for c in range(FIELDS)]
            base = [
                6.0 * mid[k, c] + ((west[c] + east[c]) + (north[c] + south[c]))
                for c in range(FIELDS)
            ]
            spread = courant * ((east[0] - west[0]) + (north[1] - south[1]))
            push_x = courant * ((east[3] - west[3]) + (east[2] - west[2]))
            push_y = courant * ((north[3] - south[3]) + (north[2] - south[2]))
            out = [base[0] - push_x, base[1] - push_y, base[2] - 0.25 * spread, base[3] - spread]
            for c in range(FIELDS):
                target[group, at + k, c, :, pl.ds(j * LANES, LANES)] = out[c]
        mid, down_before = mid_next, down
        up, down = up_next, down_next


def quarter(code):
    cosine = jnp.where(code == 0, 1.0, jnp.where(code == 2, -1.0, 0.0))
    sine = jnp.where(code == 1, 1.0, jnp.where(code == 3, -1.0, 0.0))
    return cosine.astype(f32), sine.astype(f32)


def per_level(scalars, group):
    level = lax.broadcasted_iota(jnp.int32, (GROUP, LANES), 0)
    out = jnp.zeros((GROUP, LANES), f32)
    for k in range(GROUP):
        out = jnp.where(level == k, scalars[group * GROUP + k], out)
    return out


def split(value):
    high = value.astype(bf16)
    return high, (value - high.astype(f32)).astype(bf16)


def kernel(
    n_face, n_tile, cols, halo,
    wave_in, turns_in, mass_in, counts_in, state, source, row, weight,
    fields_out, means_out,
    first, odd, even, slab, cells, picked, courants, masses, rows, weights,
    spots0, spots1, sums, inbox, wave, turns, mass, counts,
    load_sem, row_sem, weight_sem, scalar_sem, store_sem, spot_sem, send_sem, recv_sem,
    out_sem, in_sem,
):
    face, tile = lax.axis_index("face"), lax.axis_index("tile")
    devices = n_face * n_tile
    me = face * n_tile + tile
    levels = wave.shape[0]
    groups = levels // GROUP
    width = state.shape[2]
    repeat = width // LANES
    mesh_id = pl.DeviceIdType.MESH

    def place(index):
        index = lax.rem(index, devices)
        return lax.div(index, n_tile), lax.rem(index, n_tile)

    right, left = place(me + 1), place(me + devices - 1)

    def lanes_of(ref, j):
        return ref.at[:, :, pl.ds(j * LANES, LANES)]

    loads = [
        pltpu.make_async_copy(lanes_of(state, j), slab.at[:, j], load_sem.at[j])
        for j in range(repeat)
    ]
    for load in loads:
        load.start()
    row_load = pltpu.make_async_copy(row, rows, row_sem)
    row_load.start()
    weight_load = pltpu.make_async_copy(weight, weights, weight_sem)
    weight_load.start()

    scalars = [(wave_in, wave), (turns_in, turns), (mass_in, mass), (counts_in, counts)]
    scalar_loads = [
        pltpu.make_async_copy(there, here, scalar_sem.at[k])
        for k, (there, here) in enumerate(scalars)
    ]
    for scalar_load in scalar_loads:
        scalar_load.start()

    barrier = pltpu.get_barrier_semaphore()

    def greet(i, carry):
        pl.semaphore_signal(barrier, inc=1, device_id=place(me + i), device_id_type=mesh_id)
        return carry

    lax.fori_loop(1, devices, greet, 0)

    for scalar_load in scalar_loads:
        scalar_load.wait()
    for g in range(groups):
        courants[g] = 5.0 * per_level(wave, g)
        masses[g] = per_level(mass, g)

    def wide(value):
        return jnp.concatenate([value] * repeat, axis=1)

    def lift(g, x):
        for c in range(FIELDS):
            for j in range(repeat):
                lifted = slab[c, j, pl.ds(g * GROUP * cols + x, GROUP, stride=cols), :]
                lifted = 0.5 * lifted if c == 2 else lifted
                first[g, x + halo, c, :, pl.ds(j * LANES, LANES)] = lifted

    for load in loads:
        load.wait()

    def lift_edge(i, carry):
        g, j = lax.div(i, 2 * halo), lax.rem(i, 2 * halo)
        lift(g, j + (cols - 2 * halo) * lax.div(j, halo))
        return carry

    lax.fori_loop(0, groups * 2 * halo, lift_edge, 0)

    pl.semaphore_wait(barrier, devices - 1)

    messages = [(g, 1, halo) for g in range(groups - 1)]
    messages += [(groups - 1, k, 1) for k in range(1, halo + 1)]

    def halo_copy(side, m):
        g, k, count = messages[m]
        far = k + count - 1
        if side == 0:
            here, there, to = cols + halo - far, halo - far, right
        else:
            here, there, to = halo + k - 1, cols + halo + k - 1, left
        return pltpu.make_async_remote_copy(
            src_ref=first.at[g, pl.ds(here, count)],
            dst_ref=first.at[g, pl.ds(there, count)],
            send_sem=send_sem.at[side, m],
            recv_sem=recv_sem.at[side, m],
            device_id=to,
            device_id_type=mesh_id,
        )

    for m in range(len(messages)):
        for side in range(2):
            halo_copy(side, m).start()

    def lift_inner(i, carry):
        n = cols - 2 * halo
        lift(lax.div(i, n), halo + lax.rem(i, n))
        return carry

    lax.fori_loop(0, groups * (cols - 2 * halo), lift_inner, 0)

    steps = [(first, odd), (odd, even), (even, odd), (odd, even)]

    for s, (old, new) in enumerate(steps, 1):

        def inner(g, carry, old=old, new=new, s=s):
            for x in range(s, cols - s, 2):
                strip(old, new, g, x + halo, 2, courants[g])
            return carry

        lax.fori_loop(0, groups, inner, 0)

    def finish(x):
        values = {}
        for g in range(groups):
            for c in range(FIELDS):
                value = even[g, x + halo, c] * (2.0 * SCALE if c == 2 else SCALE)
                for j in range(repeat):
                    part = value[:, j * LANES : (j + 1) * LANES]
                    slab[c, j, pl.ds(g * GROUP * cols + x, GROUP, stride=cols), :] = part
                values[c, g] = value
        blocks = [values[c, g] for c in range(FIELDS) for g in range(groups)]
        blocks += [values[1, g] * (wide(masses[g]) + values[3, g]) for g in range(groups)]
        blocks.append(jnp.ones((GROUP, width), f32))
        spare = LANES - GROUP * len(blocks)
        blocks.append(jnp.zeros((spare, width), f32))
        start = pl.multiple_of(x * width, width)
        cells[pl.ds(start, width), :] = jnp.concatenate(blocks, axis=0).T

    def finish_inner(i, carry):
        finish(halo + i)
        return carry

    lax.fori_loop(0, cols - 2 * halo, finish_inner, 0)

    west_cos, west_sin = quarter(jnp.where(tile == 0, turns[face], 0))
    east_cos, east_sin = quarter(jnp.where(tile == n_tile - 1, turns[lax.rem(face + 1, n_face)], 0))

    west_turn, east_turn = (west_cos, west_sin), (east_cos, east_sin)
    for m, (g, k, count) in enumerate(messages):
        halo_copy(0, m).wait_recv()
        halo_copy(1, m).wait_recv()
        if count == halo:
            for s, (old, new) in enumerate(steps, 1):
                strip(old, new, g, s, halo, courants[g], {halo - 1 - s: west_turn})
                strip(old, new, g, cols - s + halo, halo, courants[g], {s - 1: east_turn})
            continue
        for s, (old, new) in enumerate(steps, 1):
            x = s - k
            strip(old, new, g, x + halo, 1, courants[g], {-1 - x: west_turn})
            x = cols - 1 + k - s
            strip(old, new, g, x + halo, 1, courants[g], {cols - 1 - x: east_turn})
        finish(halo - k)
        finish(cols - 1 - halo + k)

    stores = [
        pltpu.make_async_copy(slab.at[:, j], lanes_of(fields_out, j), store_sem.at[j])
        for j in range(repeat)
    ]
    for store in stores:
        store.start()

    row_load.wait()
    weight_load.wait()
    spots = (spots0, spots1)
    rounds = devices // GATHERED
    slots = rows.shape[1]

    def first_band(turn):
        return pl.multiple_of(lax.rem(lax.div(me, GATHERED) + 1 + turn, rounds) * GATHERED, GATHERED)

    def spot_copy(turn, slot):
        return pltpu.make_async_copy(
            source.at[pl.ds(first_band(turn), GATHERED)], spots[slot], spot_sem.at[slot]
        )

    def pick(slot):
        for k in range(GATHERED):
            for j in range(slots):
                picked[slot, k, pl.ds(j, 1), :] = cells[pl.ds(spots[slot][k, j], 1), :]

    sub = lax.broadcasted_iota(jnp.int32, (2 * BAND_ROWS, slots), 0)
    link = lax.broadcasted_iota(jnp.int32, (2 * BAND_ROWS, slots), 1)

    def add_up(turn, slot):
        start = first_band(turn)
        for k in range(GATHERED):
            band = start + k
            w = weights[pl.ds(band, 1), :]
            high = w.astype(bf16).astype(f32)
            part = jnp.where(sub < BAND_ROWS, high, w - high)
            mine = (rows[pl.ds(band, 1), :] == lax.rem(sub, BAND_ROWS)) & (link < counts[band])
            lhs = jnp.where(mine, part, 0.0).astype(bf16)
            high_cells, low_cells = split(picked[slot, k])
            product = jnp.dot(
                lhs,
                jnp.concatenate([high_cells, low_cells], axis=1),
                preferred_element_type=f32,
            )
            sums[band] = (
                product[:BAND_ROWS, :LANES]
                + product[:BAND_ROWS, LANES:]
                + product[BAND_ROWS:, :LANES]
            )

    def send(turn):
        start = first_band(turn)
        for k in range(GATHERED):
            band = start + k

            @pl.when(band != me)
            def _():
                pltpu.make_async_remote_copy(
                    src_ref=sums.at[band],
                    dst_ref=inbox.at[me],
                    send_sem=out_sem,
                    recv_sem=in_sem,
                    device_id=place(band),
                    device_id_type=mesh_id,
                ).start()

            @pl.when(band == me)
            def _():
                inbox[me] = sums[band]

    spot_copy(0, 0).start()
    spot_copy(1, 1).start()
    spot_copy(0, 0).wait()
    pick(0)
    spot_copy(2, 0).start()

    def two_rounds(i, carry):
        for slot in (1, 0):
            turn = 2 * i + 2 - slot
            spot_copy(turn, slot).wait()
            pick(slot)
            add_up(turn - 1, 1 - slot)

            @pl.when(turn + 2 < rounds)
            def _():
                spot_copy(turn + 2, slot).start()

            send(turn - 1)
        return carry

    lax.fori_loop(0, rounds // 2 - 1, two_rounds, 0)
    spot_copy(rounds - 1, 1).wait()
    pick(1)
    add_up(rounds - 2, 0)
    send(rounds - 2)
    add_up(rounds - 1, 1)
    send(rounds - 1)

    others = pltpu.make_async_remote_copy(
        src_ref=sums.at[pl.ds(0, devices - 1)],
        dst_ref=inbox.at[pl.ds(0, devices - 1)],
        send_sem=out_sem,
        recv_sem=in_sem,
        device_id=right,
        device_id_type=mesh_id,
    )
    others.wait_recv()
    total = jnp.sum(inbox[...], axis=0)
    ones_at = (FIELDS + 1) * levels
    means = total / jnp.broadcast_to(total[:, ones_at : ones_at + 1], total.shape)
    zonal = means
    lane = lax.broadcasted_iota(jnp.int32, means.shape, 1)
    k = 1
    while k < levels:
        means = means + jnp.where(lane >= FIELDS * levels + k, pltpu.roll(means, k, 1), 0.0)
        k *= 2
    lat_row = me * BAND_ROWS + lax.broadcasted_iota(jnp.int32, means.shape, 0)
    total_rows = BAND_ROWS * devices
    phi = ((lat_row.astype(f32) + 0.5) / total_rows - 0.5) * (jnp.pi / 2)
    stream = jnp.cos(phi) * means
    means_out[...] = jnp.where(lane < FIELDS * levels, zonal, stream)

    for m in range(len(messages)):
        for side in range(2):
            halo_copy(side, m).wait_send()
    others.wait_send()
    for store in stores:
        store.wait()


def hand_over(fields_in, means, new_state, zonal, stream, held, in_sem, out_sem):
    parts, length = held.shape[0], held.shape[2]
    per_field = parts // FIELDS

    def piece(ref, k):
        return ref.at[k // per_field, pl.ds(k % per_field * length, length)]

    loads = [
        pltpu.make_async_copy(piece(fields_in, k), held.at[k, 0], in_sem.at[k])
        for k in range(parts)
    ]
    stores = [
        pltpu.make_async_copy(held.at[k, 0], piece(new_state, k), out_sem.at[k])
        for k in range(parts)
    ]
    for load in loads:
        load.start()
    count = zonal.shape[1]
    zonal[...] = means[:, :count]
    stream[...] = means[:, count : count + stream.shape[1]]
    for load, store in zip(loads, stores):
        load.wait()
        store.start()
    for store in stores:
        store.wait()


def on_device(n_face, n_tile, state, wave, turns, mass, source, row, weight, count):
    fields, levels, cols, width = state.shape
    halo = SUBSTEPS
    groups = levels // GROUP
    devices = n_face * n_tile
    slots = source.shape[2]
    merged = (fields, levels * cols, width)
    vmem = pl.BlockSpec(memory_space=pltpu.VMEM)
    hbm = pl.BlockSpec(memory_space=pltpu.HBM)
    field = pltpu.VMEM((groups, cols + 2 * halo, fields, GROUP, width), f32)
    dma = pltpu.SemaphoreType.DMA

    def body(*refs):
        kernel(n_face, n_tile, cols, halo, *refs)

    new_fields, means = pl.pallas_call(
        body,
        out_shape=(
            jax.ShapeDtypeStruct(merged, f32),
            jax.ShapeDtypeStruct((BAND_ROWS, LANES), f32),
        ),
        in_specs=[hbm] * 8,
        out_specs=(hbm, vmem),
        scratch_shapes=[
            field,
            field,
            field,
            pltpu.VMEM((fields, width // LANES, levels * cols, LANES), f32),
            pltpu.VMEM((cols * width, LANES), f32),
            pltpu.VMEM((2, GATHERED, slots, LANES), f32),
            pltpu.VMEM((groups, GROUP, LANES), f32),
            pltpu.VMEM((groups, GROUP, LANES), f32),
            pltpu.VMEM((devices, slots), jnp.int32),
            pltpu.VMEM((devices, slots), f32),
            pltpu.SMEM((GATHERED, slots), jnp.int32),
            pltpu.SMEM((GATHERED, slots), jnp.int32),
            pltpu.VMEM((devices, BAND_ROWS, LANES), f32),
            pltpu.VMEM((devices, BAND_ROWS, LANES), f32),
            pltpu.SMEM((levels,), f32),
            pltpu.SMEM((n_face,), jnp.int32),
            pltpu.SMEM((levels,), f32),
            pltpu.SMEM((devices,), jnp.int32),
            dma((width // LANES,)),
            dma,
            dma,
            dma((4,)),
            dma((width // LANES,)),
            dma((2,)),
            dma((2, groups - 1 + halo)),
            dma((2, groups - 1 + halo)),
            dma,
            dma,
        ],
        compiler_params=pltpu.CompilerParams(
            collective_id=1, has_side_effects=True, vmem_limit_bytes=57 * 2**20
        ),
    )(
        wave,
        turns,
        mass,
        count[0],
        state.reshape(merged),
        source[0],
        row[0],
        weight[0],
    )
    new_state, zonal, stream = pl.pallas_call(
        hand_over,
        out_shape=(
            jax.ShapeDtypeStruct(merged, f32),
            jax.ShapeDtypeStruct((BAND_ROWS, fields * levels), f32),
            jax.ShapeDtypeStruct((BAND_ROWS, levels), f32),
        ),
        in_specs=[hbm, vmem],
        out_specs=(hbm, vmem, vmem),
        scratch_shapes=[
            pltpu.VMEM((HANDED, 1, fields * levels * cols // HANDED, width), f32),
            dma((HANDED,)),
            dma((HANDED,)),
        ],
        compiler_params=pltpu.CompilerParams(vmem_limit_bytes=57 * 2**20),
    )(new_fields, means)
    return new_state.reshape(state.shape), zonal, stream


def solution(mesh):
    n_face, n_tile = mesh.shape["face"], mesh.shape["tile"]
    both = ("face", "tile")
    zonal_dim = P(None, None, both, None)
    links = P(both, None, None)

    def program(*args):
        return on_device(n_face, n_tile, *args)

    return jax.shard_map(
        program,
        mesh=mesh,
        in_specs=(zonal_dim, P(), P(), P(), links, links, links, P(both, None)),
        out_specs=(zonal_dim, P(both, None), P(both, None)),
        check_vma=False,
    )
```

```python
import jax
import jax.numpy as jnp
from jax import lax
from jax.experimental import pallas as pl
from jax.experimental.pallas import tpu as pltpu
from jax.sharding import PartitionSpec as P

SUBSTEPS = 4
BAND_ROWS = 4
FIELDS = 4
GROUP = 8
LANES = 128
GATHERED = 8
HANDED = 16
SCALE = 10.0**-SUBSTEPS

f32 = jnp.float32
bf16 = jnp.bfloat16


def turned(wind, turn):
    cosine, sine = turn
    east, north = wind
    return cosine * east - sine * north, sine * east + cosine * north


def strip(source, target, group, at, count, courant, turns=None):
    turns = turns or {}
    blocks = source.shape[4] // LANES
    lane = lax.broadcasted_iota(jnp.int32, (GROUP, LANES), 1)
    first_lane, last_lane = lane == 0, lane == LANES - 1
    inside = range(count)

    def mids(j):
        return {
            (k, c): source[group, at + k, c, :, pl.ds(j * LANES, LANES)]
            for k in inside
            for c in range(FIELDS)
        }

    def rolls(mid, amount):
        return {key: pltpu.roll(q, amount, 1) for key, q in mid.items()}

    mid = mids(0)
    up, down = rolls(mid, LANES - 1), rolls(mid, 1)
    zeros = {key: jnp.zeros((GROUP, LANES), f32) for key in mid}
    down_before = zeros
    for j in range(blocks):
        if j + 1 < blocks:
            mid_next = mids(j + 1)
            up_next, down_next = rolls(mid_next, LANES - 1), rolls(mid_next, 1)
        else:
            mid_next, up_next, down_next = None, zeros, None
        here = dict(mid)
        for k in (-1, count):
            for c in range(FIELDS):
                here[k, c] = source[group, at + k, c, :, pl.ds(j * LANES, LANES)]
        for k in inside:
            west = [here[k - 1, c] for c in range(FIELDS)]
            east = [here[k + 1, c] for c in range(FIELDS)]
            if k - 1 in turns:
                west[:2] = turned(west[:2], turns[k - 1])
            if k in turns:
                cosine, sine = turns[k]
                east[:2] = turned(east[:2], (cosine, -sine))
            north = [jnp.where(last_lane, up_next[k, c], up[k, c]) for c in range(FIELDS)]
            south = [jnp.where(first_lane, down_before[k, c], down[k, c]) for c in range(FIELDS)]
            base = [
                6.0 * mid[k, c] + ((west[c] + east[c]) + (north[c] + south[c]))
                for c in range(FIELDS)
            ]
            spread = courant * ((east[0] - west[0]) + (north[1] - south[1]))
            push_x = courant * ((east[3] - west[3]) + (east[2] - west[2]))
            push_y = courant * ((north[3] - south[3]) + (north[2] - south[2]))
            out = [base[0] - push_x, base[1] - push_y, base[2] - 0.25 * spread, base[3] - spread]
            for c in range(FIELDS):
                target[group, at + k, c, :, pl.ds(j * LANES, LANES)] = out[c]
        mid, down_before = mid_next, down
        up, down = up_next, down_next


def quarter(code):
    cosine = jnp.where(code == 0, 1.0, jnp.where(code == 2, -1.0, 0.0))
    sine = jnp.where(code == 1, 1.0, jnp.where(code == 3, -1.0, 0.0))
    return cosine.astype(f32), sine.astype(f32)


def per_level(scalars, group):
    level = lax.broadcasted_iota(jnp.int32, (GROUP, LANES), 0)
    out = jnp.zeros((GROUP, LANES), f32)
    for k in range(GROUP):
        out = jnp.where(level == k, scalars[group * GROUP + k], out)
    return out


def split(value):
    high = value.astype(bf16)
    return high, (value - high.astype(f32)).astype(bf16)


def kernel(
    n_face, n_tile, cols, halo,
    wave_in, turns_in, mass_in, counts_in, state, source, row, weight,
    fields_out, means_out,
    first, odd, even, slab, cells, picked, courants, masses, rows, weights,
    spots0, spots1, sums, inbox, wave, turns, mass, counts,
    load_sem, row_sem, weight_sem, scalar_sem, store_sem, spot_sem, send_sem, recv_sem,
    out_sem, in_sem, meet,
):
    face, tile = lax.axis_index("face"), lax.axis_index("tile")
    devices = n_face * n_tile
    me = face * n_tile + tile
    levels = wave.shape[0]
    groups = levels // GROUP
    width = state.shape[2]
    repeat = width // LANES
    mesh_id = pl.DeviceIdType.MESH

    def place(index):
        index = lax.rem(index, devices)
        return lax.div(index, n_tile), lax.rem(index, n_tile)

    right, left = place(me + 1), place(me + devices - 1)

    def lanes_of(ref, j):
        return ref.at[:, :, pl.ds(j * LANES, LANES)]

    loads = [
        pltpu.make_async_copy(lanes_of(state, j), slab.at[:, j], load_sem.at[j])
        for j in range(repeat)
    ]
    for load in loads:
        load.start()
    row_load = pltpu.make_async_copy(row, rows, row_sem)
    row_load.start()
    weight_load = pltpu.make_async_copy(weight, weights, weight_sem)
    weight_load.start()

    scalars = [(wave_in, wave), (turns_in, turns), (mass_in, mass), (counts_in, counts)]
    scalar_loads = [
        pltpu.make_async_copy(there, here, scalar_sem.at[k])
        for k, (there, here) in enumerate(scalars)
    ]
    for scalar_load in scalar_loads:
        scalar_load.start()

    barrier = pltpu.get_barrier_semaphore()

    def partner(b):
        bit = lax.rem(lax.div(me, 1 << b), 2)
        return place(me + (1 - 2 * bit) * (1 << b))

    partners = devices.bit_length() - 1
    greeted = [right, left] + [partner(b) for b in range(partners)]
    for device in greeted:
        pl.semaphore_signal(barrier, inc=1, device_id=device, device_id_type=mesh_id)

    def tell(b):
        pl.semaphore_signal(meet.at[b], inc=1, device_id=partner(b), device_id_type=mesh_id)

    def hear(b):
        pl.semaphore_wait(meet.at[b], 1)

    for scalar_load in scalar_loads:
        scalar_load.wait()
    for g in range(groups):
        courants[g] = 5.0 * per_level(wave, g)
        masses[g] = per_level(mass, g)

    def wide(value):
        return jnp.concatenate([value] * repeat, axis=1)

    def lift(g, x):
        for c in range(FIELDS):
            for j in range(repeat):
                lifted = slab[c, j, pl.ds(g * GROUP * cols + x, GROUP, stride=cols), :]
                lifted = 0.5 * lifted if c == 2 else lifted
                first[g, x + halo, c, :, pl.ds(j * LANES, LANES)] = lifted

    for load in loads:
        load.wait()

    def lift_edge(i, carry):
        g, j = lax.div(i, 2 * halo), lax.rem(i, 2 * halo)
        lift(g, j + (cols - 2 * halo) * lax.div(j, halo))
        return carry

    lax.fori_loop(0, groups * 2 * halo, lift_edge, 0)

    pl.semaphore_wait(barrier, len(greeted))

    messages = [(g, 1, halo) for g in range(groups - 1)]
    messages += [(groups - 1, k, 1) for k in range(1, halo + 1)]

    def halo_copy(side, m):
        g, k, count = messages[m]
        far = k + count - 1
        if side == 0:
            here, there, to = cols + halo - far, halo - far, right
        else:
            here, there, to = halo + k - 1, cols + halo + k - 1, left
        return pltpu.make_async_remote_copy(
            src_ref=first.at[g, pl.ds(here, count)],
            dst_ref=first.at[g, pl.ds(there, count)],
            send_sem=send_sem.at[side, m],
            recv_sem=recv_sem.at[side, m],
            device_id=to,
            device_id_type=mesh_id,
        )

    for m in range(len(messages)):
        for side in range(2):
            halo_copy(side, m).start()
    tell(0)
    met = 0

    spots = (spots0, spots1)
    rounds = devices // GATHERED
    slots = rows.shape[1]

    def first_band(turn):
        return pl.multiple_of(lax.rem(lax.div(me, GATHERED) + 1 + turn, rounds) * GATHERED, GATHERED)

    def spot_copy(turn, slot):
        return pltpu.make_async_copy(
            source.at[pl.ds(first_band(turn), GATHERED)], spots[slot], spot_sem.at[slot]
        )

    def lift_inner(i, carry):
        n = cols - 2 * halo
        lift(lax.div(i, n), halo + lax.rem(i, n))
        return carry

    lax.fori_loop(0, groups * (cols - 2 * halo), lift_inner, 0)
    spot_copy(0, 0).start()
    spot_copy(1, 1).start()

    steps = [(first, odd), (odd, even), (even, odd), (odd, even)]

    for s, (old, new) in enumerate(steps, 1):

        def inner(g, carry, old=old, new=new, s=s):
            for x in range(s, cols - s, 2):
                strip(old, new, g, x + halo, 2, courants[g])
            return carry

        lax.fori_loop(0, groups, inner, 0)
        if met + 1 < partners:
            hear(met)
            met += 1
            tell(met)

    def finish(x):
        values = {}
        for g in range(groups):
            for c in range(FIELDS):
                value = even[g, x + halo, c] * (2.0 * SCALE if c == 2 else SCALE)
                for j in range(repeat):
                    part = value[:, j * LANES : (j + 1) * LANES]
                    slab[c, j, pl.ds(g * GROUP * cols + x, GROUP, stride=cols), :] = part
                values[c, g] = value
        blocks = [values[c, g] for c in range(FIELDS) for g in range(groups)]
        blocks += [values[1, g] * (wide(masses[g]) + values[3, g]) for g in range(groups)]
        blocks.append(jnp.ones((GROUP, width), f32))
        spare = LANES - GROUP * len(blocks)
        blocks.append(jnp.zeros((spare, width), f32))
        start = pl.multiple_of(x * width, width)
        cells[pl.ds(start, width), :] = jnp.concatenate(blocks, axis=0).T

    def finish_inner(i, carry):
        finish(halo + i)
        return carry

    lax.fori_loop(0, cols - 2 * halo, finish_inner, 0)

    while met + 1 < partners:
        hear(met)
        met += 1
        tell(met)

    west_cos, west_sin = quarter(jnp.where(tile == 0, turns[face], 0))
    east_cos, east_sin = quarter(jnp.where(tile == n_tile - 1, turns[lax.rem(face + 1, n_face)], 0))

    west_turn, east_turn = (west_cos, west_sin), (east_cos, east_sin)
    for m, (g, k, count) in enumerate(messages):
        halo_copy(0, m).wait_recv()
        halo_copy(1, m).wait_recv()
        if count == halo:
            for s, (old, new) in enumerate(steps, 1):
                strip(old, new, g, s, halo, courants[g], {halo - 1 - s: west_turn})
                strip(old, new, g, cols - s + halo, halo, courants[g], {s - 1: east_turn})
            continue
        for s, (old, new) in enumerate(steps, 1):
            x = s - k
            strip(old, new, g, x + halo, 1, courants[g], {-1 - x: west_turn})
            x = cols - 1 + k - s
            strip(old, new, g, x + halo, 1, courants[g], {cols - 1 - x: east_turn})
        finish(halo - k)
        finish(cols - 1 - halo + k)

    stores = [
        pltpu.make_async_copy(slab.at[:, j], lanes_of(fields_out, j), store_sem.at[j])
        for j in range(repeat)
    ]
    for store in stores:
        store.start()

    row_load.wait()
    weight_load.wait()
    hear(met)
    def pick(slot):
        for k in range(GATHERED):
            for j in range(slots):
                picked[slot, k, pl.ds(j, 1), :] = cells[pl.ds(spots[slot][k, j], 1), :]

    sub = lax.broadcasted_iota(jnp.int32, (2 * BAND_ROWS, slots), 0)
    link = lax.broadcasted_iota(jnp.int32, (2 * BAND_ROWS, slots), 1)

    def add_up(turn, slot):
        start = first_band(turn)
        for k in range(GATHERED):
            band = start + k
            w = weights[pl.ds(band, 1), :]
            high = w.astype(bf16).astype(f32)
            part = jnp.where(sub < BAND_ROWS, high, w - high)
            mine = (rows[pl.ds(band, 1), :] == lax.rem(sub, BAND_ROWS)) & (link < counts[band])
            lhs = jnp.where(mine, part, 0.0).astype(bf16)
            high_cells, low_cells = split(picked[slot, k])
            product = jnp.dot(
                lhs,
                jnp.concatenate([high_cells, low_cells], axis=1),
                preferred_element_type=f32,
            )
            sums[band] = (
                product[:BAND_ROWS, :LANES]
                + product[:BAND_ROWS, LANES:]
                + product[BAND_ROWS:, :LANES]
            )

    def send(turn):
        start = first_band(turn)
        for k in range(GATHERED):
            band = start + k

            @pl.when(band != me)
            def _():
                pltpu.make_async_remote_copy(
                    src_ref=sums.at[band],
                    dst_ref=inbox.at[me],
                    send_sem=out_sem,
                    recv_sem=in_sem,
                    device_id=place(band),
                    device_id_type=mesh_id,
                ).start()

            @pl.when(band == me)
            def _():
                inbox[me] = sums[band]

    spot_copy(0, 0).wait()
    pick(0)
    spot_copy(2, 0).start()

    def two_rounds(i, carry):
        for slot in (1, 0):
            turn = 2 * i + 2 - slot
            spot_copy(turn, slot).wait()
            pick(slot)
            add_up(turn - 1, 1 - slot)

            @pl.when(turn + 2 < rounds)
            def _():
                spot_copy(turn + 2, slot).start()

            send(turn - 1)
        return carry

    lax.fori_loop(0, rounds // 2 - 1, two_rounds, 0)
    spot_copy(rounds - 1, 1).wait()
    pick(1)
    add_up(rounds - 2, 0)
    send(rounds - 2)
    add_up(rounds - 1, 1)
    send(rounds - 1)

    others = pltpu.make_async_remote_copy(
        src_ref=sums.at[pl.ds(0, devices - 1)],
        dst_ref=inbox.at[pl.ds(0, devices - 1)],
        send_sem=out_sem,
        recv_sem=in_sem,
        device_id=right,
        device_id_type=mesh_id,
    )
    lat_row = me * BAND_ROWS + lax.broadcasted_iota(jnp.int32, (BAND_ROWS, LANES), 0)
    total_rows = BAND_ROWS * devices
    phi = ((lat_row.astype(f32) + 0.5) / total_rows - 0.5) * (jnp.pi / 2)
    cosine = jnp.cos(phi)
    others.wait_recv()
    total = jnp.sum(inbox[...], axis=0)
    ones_at = (FIELDS + 1) * levels
    means = total / jnp.broadcast_to(total[:, ones_at : ones_at + 1], total.shape)
    zonal = means
    lane = lax.broadcasted_iota(jnp.int32, means.shape, 1)
    k = 1
    while k < levels:
        means = means + jnp.where(lane >= FIELDS * levels + k, pltpu.roll(means, k, 1), 0.0)
        k *= 2
    stream = cosine * means
    means_out[...] = jnp.where(lane < FIELDS * levels, zonal, stream)

    for m in range(len(messages)):
        for side in range(2):
            halo_copy(side, m).wait_send()
    others.wait_send()
    for store in stores:
        store.wait()


def hand_over(fields_in, means, new_state, zonal, stream, held, in_sem, out_sem):
    parts, length = held.shape[0], held.shape[2]
    per_field = parts // FIELDS

    def piece(ref, k):
        return ref.at[k // per_field, pl.ds(k % per_field * length, length)]

    loads = [
        pltpu.make_async_copy(piece(fields_in, k), held.at[k, 0], in_sem.at[k])
        for k in range(parts)
    ]
    stores = [
        pltpu.make_async_copy(held.at[k, 0], piece(new_state, k), out_sem.at[k])
        for k in range(parts)
    ]
    for load in loads:
        load.start()
    count = zonal.shape[1]
    zonal[...] = means[:, :count]
    stream[...] = means[:, count : count + stream.shape[1]]
    for load, store in zip(loads, stores):
        load.wait()
        store.start()
    for store in stores:
        store.wait()


def on_device(n_face, n_tile, state, wave, turns, mass, source, row, weight, count):
    fields, levels, cols, width = state.shape
    halo = SUBSTEPS
    groups = levels // GROUP
    devices = n_face * n_tile
    slots = source.shape[2]
    merged = (fields, levels * cols, width)
    vmem = pl.BlockSpec(memory_space=pltpu.VMEM)
    hbm = pl.BlockSpec(memory_space=pltpu.HBM)
    field = pltpu.VMEM((groups, cols + 2 * halo, fields, GROUP, width), f32)
    dma = pltpu.SemaphoreType.DMA

    def body(*refs):
        kernel(n_face, n_tile, cols, halo, *refs)

    new_fields, means = pl.pallas_call(
        body,
        out_shape=(
            jax.ShapeDtypeStruct(merged, f32),
            jax.ShapeDtypeStruct((BAND_ROWS, LANES), f32),
        ),
        in_specs=[hbm] * 8,
        out_specs=(hbm, vmem),
        scratch_shapes=[
            field,
            field,
            field,
            pltpu.VMEM((fields, width // LANES, levels * cols, LANES), f32),
            pltpu.VMEM((cols * width, LANES), f32),
            pltpu.VMEM((2, GATHERED, slots, LANES), f32),
            pltpu.VMEM((groups, GROUP, LANES), f32),
            pltpu.VMEM((groups, GROUP, LANES), f32),
            pltpu.VMEM((devices, slots), jnp.int32),
            pltpu.VMEM((devices, slots), f32),
            pltpu.SMEM((GATHERED, slots), jnp.int32),
            pltpu.SMEM((GATHERED, slots), jnp.int32),
            pltpu.VMEM((devices, BAND_ROWS, LANES), f32),
            pltpu.VMEM((devices, BAND_ROWS, LANES), f32),
            pltpu.SMEM((levels,), f32),
            pltpu.SMEM((n_face,), jnp.int32),
            pltpu.SMEM((levels,), f32),
            pltpu.SMEM((devices,), jnp.int32),
            dma((width // LANES,)),
            dma,
            dma,
            dma((4,)),
            dma((width // LANES,)),
            dma((2,)),
            dma((2, groups - 1 + halo)),
            dma((2, groups - 1 + halo)),
            dma,
            dma,
            pltpu.SemaphoreType.REGULAR((devices.bit_length() - 1,)),
        ],
        compiler_params=pltpu.CompilerParams(
            collective_id=1, has_side_effects=True, vmem_limit_bytes=57 * 2**20
        ),
    )(
        wave,
        turns,
        mass,
        count[0],
        state.reshape(merged),
        source[0],
        row[0],
        weight[0],
    )
    new_state, zonal, stream = pl.pallas_call(
        hand_over,
        out_shape=(
            jax.ShapeDtypeStruct(merged, f32),
            jax.ShapeDtypeStruct((BAND_ROWS, fields * levels), f32),
            jax.ShapeDtypeStruct((BAND_ROWS, levels), f32),
        ),
        in_specs=[hbm, vmem],
        out_specs=(hbm, vmem, vmem),
        scratch_shapes=[
            pltpu.VMEM((HANDED, 1, fields * levels * cols // HANDED, width), f32),
            dma((HANDED,)),
            dma((HANDED,)),
        ],
        compiler_params=pltpu.CompilerParams(vmem_limit_bytes=57 * 2**20),
    )(new_fields, means)
    return new_state.reshape(state.shape), zonal, stream


def solution(mesh):
    n_face, n_tile = mesh.shape["face"], mesh.shape["tile"]
    both = ("face", "tile")
    zonal_dim = P(None, None, both, None)
    links = P(both, None, None)

    def program(*args):
        return on_device(n_face, n_tile, *args)

    return jax.shard_map(
        program,
        mesh=mesh,
        in_specs=(zonal_dim, P(), P(), P(), links, links, links, P(both, None)),
        out_specs=(zonal_dim, P(both, None), P(both, None)),
        check_vma=False,
    )
```

```python
import jax
import jax.numpy as jnp
from jax import lax
from jax.experimental import pallas as pl
from jax.experimental.pallas import tpu as pltpu
from jax.sharding import PartitionSpec as P

SUBSTEPS = 4
BAND_ROWS = 4
FIELDS = 4
GROUP = 8
LANES = 128
GATHERED = 8
HANDED = 16
SCALE = 10.0**-SUBSTEPS

f32 = jnp.float32
bf16 = jnp.bfloat16


def turned(wind, turn):
    cosine, sine = turn
    east, north = wind
    return cosine * east - sine * north, sine * east + cosine * north


def strip(source, target, group, at, count, courant, turns=None):
    turns = turns or {}
    blocks = source.shape[4] // LANES
    lane = lax.broadcasted_iota(jnp.int32, (GROUP, LANES), 1)
    first_lane, last_lane = lane == 0, lane == LANES - 1
    inside = range(count)

    def mids(j):
        return {
            (k, c): source[group, at + k, c, :, pl.ds(j * LANES, LANES)]
            for k in inside
            for c in range(FIELDS)
        }

    def rolls(mid, amount):
        return {key: pltpu.roll(q, amount, 1) for key, q in mid.items()}

    mid = mids(0)
    up, down = rolls(mid, LANES - 1), rolls(mid, 1)
    zeros = {key: jnp.zeros((GROUP, LANES), f32) for key in mid}
    down_before = zeros
    for j in range(blocks):
        if j + 1 < blocks:
            mid_next = mids(j + 1)
            up_next, down_next = rolls(mid_next, LANES - 1), rolls(mid_next, 1)
        else:
            mid_next, up_next, down_next = None, zeros, None
        here = dict(mid)
        for k in (-1, count):
            for c in range(FIELDS):
                here[k, c] = source[group, at + k, c, :, pl.ds(j * LANES, LANES)]
        for k in inside:
            west = [here[k - 1, c] for c in range(FIELDS)]
            east = [here[k + 1, c] for c in range(FIELDS)]
            if k - 1 in turns:
                west[:2] = turned(west[:2], turns[k - 1])
            if k in turns:
                cosine, sine = turns[k]
                east[:2] = turned(east[:2], (cosine, -sine))
            north = [jnp.where(last_lane, up_next[k, c], up[k, c]) for c in range(FIELDS)]
            south = [jnp.where(first_lane, down_before[k, c], down[k, c]) for c in range(FIELDS)]
            base = [
                6.0 * mid[k, c] + ((west[c] + east[c]) + (north[c] + south[c]))
                for c in range(FIELDS)
            ]
            spread = courant * ((east[0] - west[0]) + (north[1] - south[1]))
            push_x = courant * ((east[3] - west[3]) + (east[2] - west[2]))
            push_y = courant * ((north[3] - south[3]) + (north[2] - south[2]))
            out = [base[0] - push_x, base[1] - push_y, base[2] - 0.25 * spread, base[3] - spread]
            for c in range(FIELDS):
                target[group, at + k, c, :, pl.ds(j * LANES, LANES)] = out[c]
        mid, down_before = mid_next, down
        up, down = up_next, down_next


def quarter(code):
    cosine = jnp.where(code == 0, 1.0, jnp.where(code == 2, -1.0, 0.0))
    sine = jnp.where(code == 1, 1.0, jnp.where(code == 3, -1.0, 0.0))
    return cosine.astype(f32), sine.astype(f32)


def per_level(scalars, group):
    level = lax.broadcasted_iota(jnp.int32, (GROUP, LANES), 0)
    out = jnp.zeros((GROUP, LANES), f32)
    for k in range(GROUP):
        out = jnp.where(level == k, scalars[group * GROUP + k], out)
    return out


def split(value):
    high = value.astype(bf16)
    return high, (value - high.astype(f32)).astype(bf16)


def kernel(
    n_face, n_tile, cols, halo,
    wave_in, turns_in, mass_in, counts_in, state, source, row, weight,
    fields_out, means_out,
    first, odd, even, slab, cells, picked, courants, masses, rows, weights,
    spots0, spots1, sums, inbox, wave, turns, mass, counts,
    load_sem, row_sem, weight_sem, scalar_sem, store_sem, spot_sem, send_sem, recv_sem,
    out_sem, in_sem, meet,
):
    face, tile = lax.axis_index("face"), lax.axis_index("tile")
    devices = n_face * n_tile
    me = face * n_tile + tile
    levels = wave.shape[0]
    groups = levels // GROUP
    width = state.shape[2]
    repeat = width // LANES
    mesh_id = pl.DeviceIdType.MESH

    def place(index):
        index = lax.rem(index, devices)
        return lax.div(index, n_tile), lax.rem(index, n_tile)

    right, left = place(me + 1), place(me + devices - 1)

    def lanes_of(ref, j):
        return ref.at[:, :, pl.ds(j * LANES, LANES)]

    loads = [
        pltpu.make_async_copy(lanes_of(state, j), slab.at[:, j], load_sem.at[j])
        for j in range(repeat)
    ]
    for load in loads:
        load.start()
    row_load = pltpu.make_async_copy(row, rows, row_sem)
    row_load.start()
    weight_load = pltpu.make_async_copy(weight, weights, weight_sem)
    weight_load.start()

    scalars = [(wave_in, wave), (turns_in, turns), (mass_in, mass), (counts_in, counts)]
    scalar_loads = [
        pltpu.make_async_copy(there, here, scalar_sem.at[k])
        for k, (there, here) in enumerate(scalars)
    ]
    for scalar_load in scalar_loads:
        scalar_load.start()

    barrier = pltpu.get_barrier_semaphore()

    def partner(b):
        bit = lax.rem(lax.div(me, 1 << b), 2)
        return place(me + (1 - 2 * bit) * (1 << b))

    partners = devices.bit_length() - 1
    greeted = [right, left] + [partner(b) for b in range(partners)]
    for device in greeted:
        pl.semaphore_signal(barrier, inc=1, device_id=device, device_id_type=mesh_id)

    def tell(b):
        pl.semaphore_signal(meet.at[b], inc=1, device_id=partner(b), device_id_type=mesh_id)

    def hear(b):
        pl.semaphore_wait(meet.at[b], 1)

    for scalar_load in scalar_loads:
        scalar_load.wait()
    for g in range(groups):
        courants[g] = 5.0 * per_level(wave, g)
        masses[g] = per_level(mass, g)

    def wide(value):
        return jnp.concatenate([value] * repeat, axis=1)

    def lift(g, x):
        for c in range(FIELDS):
            for j in range(repeat):
                lifted = slab[c, j, pl.ds(g * GROUP * cols + x, GROUP, stride=cols), :]
                lifted = 0.5 * lifted if c == 2 else lifted
                first[g, x + halo, c, :, pl.ds(j * LANES, LANES)] = lifted

    for load in loads:
        load.wait()

    def lift_edge(i, carry):
        g, j = lax.div(i, 2 * halo), lax.rem(i, 2 * halo)
        lift(g, j + (cols - 2 * halo) * lax.div(j, halo))
        return carry

    lax.fori_loop(0, groups * 2 * halo, lift_edge, 0)

    pl.semaphore_wait(barrier, len(greeted))

    messages = [(g, 1, halo) for g in range(groups - 1)]
    messages += [(groups - 1, k, 1) for k in range(1, halo + 1)]

    def halo_copy(side, m):
        g, k, count = messages[m]
        far = k + count - 1
        if side == 0:
            here, there, to = cols + halo - far, halo - far, right
        else:
            here, there, to = halo + k - 1, cols + halo + k - 1, left
        return pltpu.make_async_remote_copy(
            src_ref=first.at[g, pl.ds(here, count)],
            dst_ref=first.at[g, pl.ds(there, count)],
            send_sem=send_sem.at[side, m],
            recv_sem=recv_sem.at[side, m],
            device_id=to,
            device_id_type=mesh_id,
        )

    for m in range(len(messages)):
        for side in range(2):
            halo_copy(side, m).start()
    tell(0)
    met = 0

    spots = (spots0, spots1)
    rounds = devices // GATHERED
    slots = rows.shape[1]

    def first_band(turn):
        return pl.multiple_of(lax.rem(lax.div(me, GATHERED) + 1 + turn, rounds) * GATHERED, GATHERED)

    def spot_copy(turn, slot):
        return pltpu.make_async_copy(
            source.at[pl.ds(first_band(turn), GATHERED)], spots[slot], spot_sem.at[slot]
        )

    def lift_inner(i, carry):
        n = cols - 2 * halo
        lift(lax.div(i, n), halo + lax.rem(i, n))
        return carry

    lax.fori_loop(0, groups * (cols - 2 * halo), lift_inner, 0)
    spot_copy(0, 0).start()
    spot_copy(1, 1).start()

    steps = [(first, odd), (odd, even), (even, odd), (odd, even)]

    for s, (old, new) in enumerate(steps, 1):

        def inner(g, carry, old=old, new=new, s=s):
            for x in range(s, cols - s, 2):
                strip(old, new, g, x + halo, 2, courants[g])
            return carry

        lax.fori_loop(0, groups, inner, 0)
        if met + 1 < partners:
            hear(met)
            met += 1
            tell(met)

    def finish(x):
        values = {}
        for g in range(groups):
            for c in range(FIELDS):
                value = even[g, x + halo, c] * (2.0 * SCALE if c == 2 else SCALE)
                for j in range(repeat):
                    part = value[:, j * LANES : (j + 1) * LANES]
                    slab[c, j, pl.ds(g * GROUP * cols + x, GROUP, stride=cols), :] = part
                values[c, g] = value
        blocks = [values[c, g] for c in range(FIELDS) for g in range(groups)]
        blocks += [values[1, g] * (wide(masses[g]) + values[3, g]) for g in range(groups)]
        blocks.append(jnp.ones((GROUP, width), f32))
        spare = LANES - GROUP * len(blocks)
        blocks.append(jnp.zeros((spare, width), f32))
        start = pl.multiple_of(x * width, width)
        cells[pl.ds(start, width), :] = jnp.concatenate(blocks, axis=0).T

    def finish_inner(i, carry):
        finish(halo + i)
        return carry

    lax.fori_loop(0, cols - 2 * halo, finish_inner, 0)

    while met + 1 < partners:
        hear(met)
        met += 1
        tell(met)

    west_cos, west_sin = quarter(jnp.where(tile == 0, turns[face], 0))
    east_cos, east_sin = quarter(jnp.where(tile == n_tile - 1, turns[lax.rem(face + 1, n_face)], 0))

    west_turn, east_turn = (west_cos, west_sin), (east_cos, east_sin)
    for m, (g, k, count) in enumerate(messages):
        halo_copy(0, m).wait_recv()
        halo_copy(1, m).wait_recv()
        if count == halo:
            for s, (old, new) in enumerate(steps, 1):
                strip(old, new, g, s, halo, courants[g], {halo - 1 - s: west_turn})
                strip(old, new, g, cols - s + halo, halo, courants[g], {s - 1: east_turn})
            continue
        for s, (old, new) in enumerate(steps, 1):
            x = s - k
            strip(old, new, g, x + halo, 1, courants[g], {-1 - x: west_turn})
            x = cols - 1 + k - s
            strip(old, new, g, x + halo, 1, courants[g], {cols - 1 - x: east_turn})
        finish(halo - k)
        finish(cols - 1 - halo + k)

    stores = [
        pltpu.make_async_copy(slab.at[:, j], lanes_of(fields_out, j), store_sem.at[j])
        for j in range(repeat)
    ]
    for store in stores:
        store.start()

    row_load.wait()
    weight_load.wait()
    hear(met)
    def pick(slot):
        for k in range(GATHERED):
            for j in range(slots):
                picked[slot, k, pl.ds(j, 1), :] = cells[pl.ds(spots[slot][k, j], 1), :]

    sub = lax.broadcasted_iota(jnp.int32, (2 * BAND_ROWS, slots), 0)
    link = lax.broadcasted_iota(jnp.int32, (2 * BAND_ROWS, slots), 1)

    def add_up(turn, slot):
        start = first_band(turn)
        for k in range(GATHERED):
            band = start + k
            w = weights[pl.ds(band, 1), :]
            high = w.astype(bf16).astype(f32)
            part = jnp.where(sub < BAND_ROWS, high, w - high)
            mine = (rows[pl.ds(band, 1), :] == lax.rem(sub, BAND_ROWS)) & (link < counts[band])
            lhs = jnp.where(mine, part, 0.0).astype(bf16)
            high_cells, low_cells = split(picked[slot, k])
            product = jnp.dot(
                lhs,
                jnp.concatenate([high_cells, low_cells], axis=1),
                preferred_element_type=f32,
            )
            sums[band] = (
                product[:BAND_ROWS, :LANES]
                + product[:BAND_ROWS, LANES:]
                + product[BAND_ROWS:, :LANES]
            )

    def send_band(band):
        pltpu.make_async_remote_copy(
            src_ref=sums.at[band],
            dst_ref=inbox.at[me],
            send_sem=out_sem,
            recv_sem=in_sem,
            device_id=place(band),
            device_id_type=mesh_id,
        ).start()

    def send(turn):
        for k in range(GATHERED):
            send_band(first_band(turn) + k)

    def send_last():
        for k in range(1, GATHERED):
            send_band(first_band(rounds - 1) + lax.rem(me + k, GATHERED))
        inbox[me] = sums[me]

    spot_copy(0, 0).wait()
    pick(0)
    spot_copy(2, 0).start()

    def two_rounds(i, carry):
        for slot in (1, 0):
            turn = 2 * i + 2 - slot
            spot_copy(turn, slot).wait()
            pick(slot)
            add_up(turn - 1, 1 - slot)

            @pl.when(turn + 2 < rounds)
            def _():
                spot_copy(turn + 2, slot).start()

            send(turn - 1)
        return carry

    lax.fori_loop(0, rounds // 2 - 1, two_rounds, 0)
    spot_copy(rounds - 1, 1).wait()
    pick(1)
    add_up(rounds - 2, 0)
    send(rounds - 2)
    add_up(rounds - 1, 1)
    send_last()

    others = pltpu.make_async_remote_copy(
        src_ref=sums.at[pl.ds(0, devices - 1)],
        dst_ref=inbox.at[pl.ds(0, devices - 1)],
        send_sem=out_sem,
        recv_sem=in_sem,
        device_id=right,
        device_id_type=mesh_id,
    )
    lat_row = me * BAND_ROWS + lax.broadcasted_iota(jnp.int32, (BAND_ROWS, LANES), 0)
    total_rows = BAND_ROWS * devices
    phi = ((lat_row.astype(f32) + 0.5) / total_rows - 0.5) * (jnp.pi / 2)
    cosine = jnp.cos(phi)
    others.wait_recv()
    total = jnp.sum(inbox[...], axis=0)
    ones_at = (FIELDS + 1) * levels
    means = total / jnp.broadcast_to(total[:, ones_at : ones_at + 1], total.shape)
    zonal = means
    lane = lax.broadcasted_iota(jnp.int32, means.shape, 1)
    k = 1
    while k < levels:
        means = means + jnp.where(lane >= FIELDS * levels + k, pltpu.roll(means, k, 1), 0.0)
        k *= 2
    stream = cosine * means
    means_out[...] = jnp.where(lane < FIELDS * levels, zonal, stream)

    for m in range(len(messages)):
        for side in range(2):
            halo_copy(side, m).wait_send()
    others.wait_send()
    for store in stores:
        store.wait()


def hand_over(
    fields_in, means_in, new_state, zonal_out, stream_out,
    held, means, zonal, stream, in_sem, out_sem, small_sem,
):
    parts, length = held.shape[0], held.shape[2]
    per_field = parts // FIELDS

    def piece(ref, k):
        return ref.at[k // per_field, pl.ds(k % per_field * length, length)]

    loads = [
        pltpu.make_async_copy(piece(fields_in, k), held.at[k, 0], in_sem.at[k])
        for k in range(parts)
    ]
    stores = [
        pltpu.make_async_copy(held.at[k, 0], piece(new_state, k), out_sem.at[k])
        for k in range(parts)
    ]
    load_means = pltpu.make_async_copy(means_in, means, small_sem.at[0])
    store_zonal = pltpu.make_async_copy(zonal, zonal_out, small_sem.at[1])
    store_stream = pltpu.make_async_copy(stream, stream_out, small_sem.at[2])
    load_means.start()
    for load in loads:
        load.start()
    load_means.wait()
    count = zonal.shape[1]
    zonal[...] = means[:, :count]
    stream[...] = means[:, count : count + stream.shape[1]]
    store_zonal.start()
    store_stream.start()
    for load, store in zip(loads, stores):
        load.wait()
        store.start()
    for store in [store_zonal, store_stream, *stores]:
        store.wait()


def on_device(n_face, n_tile, state, wave, turns, mass, source, row, weight, count):
    fields, levels, cols, width = state.shape
    halo = SUBSTEPS
    groups = levels // GROUP
    devices = n_face * n_tile
    slots = source.shape[2]
    merged = (fields, levels * cols, width)
    vmem = pl.BlockSpec(memory_space=pltpu.VMEM)
    hbm = pl.BlockSpec(memory_space=pltpu.HBM)
    field = pltpu.VMEM((groups, cols + 2 * halo, fields, GROUP, width), f32)
    dma = pltpu.SemaphoreType.DMA

    def body(*refs):
        kernel(n_face, n_tile, cols, halo, *refs)

    new_fields, means = pl.pallas_call(
        body,
        out_shape=(
            jax.ShapeDtypeStruct(merged, f32),
            jax.ShapeDtypeStruct((BAND_ROWS, LANES), f32),
        ),
        in_specs=[hbm] * 8,
        out_specs=(hbm, vmem),
        scratch_shapes=[
            field,
            field,
            field,
            pltpu.VMEM((fields, width // LANES, levels * cols, LANES), f32),
            pltpu.VMEM((cols * width, LANES), f32),
            pltpu.VMEM((2, GATHERED, slots, LANES), f32),
            pltpu.VMEM((groups, GROUP, LANES), f32),
            pltpu.VMEM((groups, GROUP, LANES), f32),
            pltpu.VMEM((devices, slots), jnp.int32),
            pltpu.VMEM((devices, slots), f32),
            pltpu.SMEM((GATHERED, slots), jnp.int32),
            pltpu.SMEM((GATHERED, slots), jnp.int32),
            pltpu.VMEM((devices, BAND_ROWS, LANES), f32),
            pltpu.VMEM((devices, BAND_ROWS, LANES), f32),
            pltpu.SMEM((levels,), f32),
            pltpu.SMEM((n_face,), jnp.int32),
            pltpu.SMEM((levels,), f32),
            pltpu.SMEM((devices,), jnp.int32),
            dma((width // LANES,)),
            dma,
            dma,
            dma((4,)),
            dma((width // LANES,)),
            dma((2,)),
            dma((2, groups - 1 + halo)),
            dma((2, groups - 1 + halo)),
            dma,
            dma,
            pltpu.SemaphoreType.REGULAR((devices.bit_length() - 1,)),
        ],
        compiler_params=pltpu.CompilerParams(
            collective_id=1, has_side_effects=True, vmem_limit_bytes=57 * 2**20
        ),
    )(
        wave,
        turns,
        mass,
        count[0],
        state.reshape(merged),
        source[0],
        row[0],
        weight[0],
    )
    new_state, zonal, stream = pl.pallas_call(
        hand_over,
        out_shape=(
            jax.ShapeDtypeStruct(merged, f32),
            jax.ShapeDtypeStruct((BAND_ROWS, fields * levels), f32),
            jax.ShapeDtypeStruct((BAND_ROWS, levels), f32),
        ),
        in_specs=[hbm, hbm],
        out_specs=(hbm, hbm, hbm),
        scratch_shapes=[
            pltpu.VMEM((HANDED, 1, fields * levels * cols // HANDED, width), f32),
            pltpu.VMEM((BAND_ROWS, LANES), f32),
            pltpu.VMEM((BAND_ROWS, fields * levels), f32),
            pltpu.VMEM((BAND_ROWS, levels), f32),
            dma((HANDED,)),
            dma((HANDED,)),
            dma((3,)),
        ],
        compiler_params=pltpu.CompilerParams(vmem_limit_bytes=57 * 2**20),
    )(new_fields, means)
    return new_state.reshape(state.shape), zonal, stream


def solution(mesh):
    n_face, n_tile = mesh.shape["face"], mesh.shape["tile"]
    both = ("face", "tile")
    zonal_dim = P(None, None, both, None)
    links = P(both, None, None)

    def program(*args):
        return on_device(n_face, n_tile, *args)

    return jax.shard_map(
        program,
        mesh=mesh,
        in_specs=(zonal_dim, P(), P(), P(), links, links, links, P(both, None)),
        out_specs=(zonal_dim, P(both, None), P(both, None)),
        check_vma=False,
    )
```

```python
import jax
import jax.numpy as jnp
from jax import lax
from jax.experimental import pallas as pl
from jax.experimental.pallas import tpu as pltpu
from jax.sharding import PartitionSpec as P

SUBSTEPS = 4
BAND_ROWS = 4
FIELDS = 4
GROUP = 8
LANES = 128
GATHERED = 8
HANDED = 4
SCALE = 10.0**-SUBSTEPS

f32 = jnp.float32
bf16 = jnp.bfloat16


def turned(wind, turn):
    cosine, sine = turn
    east, north = wind
    return cosine * east - sine * north, sine * east + cosine * north


def strip(source, target, group, at, count, courant, turns=None):
    turns = turns or {}
    blocks = source.shape[4] // LANES
    lane = lax.broadcasted_iota(jnp.int32, (GROUP, LANES), 1)
    first_lane, last_lane = lane == 0, lane == LANES - 1
    inside = range(count)

    def mids(j):
        return {
            (k, c): source[group, at + k, c, :, pl.ds(j * LANES, LANES)]
            for k in inside
            for c in range(FIELDS)
        }

    def rolls(mid, amount):
        return {key: pltpu.roll(q, amount, 1) for key, q in mid.items()}

    mid = mids(0)
    up, down = rolls(mid, LANES - 1), rolls(mid, 1)
    zeros = {key: jnp.zeros((GROUP, LANES), f32) for key in mid}
    down_before = zeros
    for j in range(blocks):
        if j + 1 < blocks:
            mid_next = mids(j + 1)
            up_next, down_next = rolls(mid_next, LANES - 1), rolls(mid_next, 1)
        else:
            mid_next, up_next, down_next = None, zeros, None
        here = dict(mid)
        for k in (-1, count):
            for c in range(FIELDS):
                here[k, c] = source[group, at + k, c, :, pl.ds(j * LANES, LANES)]
        for k in inside:
            west = [here[k - 1, c] for c in range(FIELDS)]
            east = [here[k + 1, c] for c in range(FIELDS)]
            if k - 1 in turns:
                west[:2] = turned(west[:2], turns[k - 1])
            if k in turns:
                cosine, sine = turns[k]
                east[:2] = turned(east[:2], (cosine, -sine))
            north = [jnp.where(last_lane, up_next[k, c], up[k, c]) for c in range(FIELDS)]
            south = [jnp.where(first_lane, down_before[k, c], down[k, c]) for c in range(FIELDS)]
            base = [
                6.0 * mid[k, c] + ((west[c] + east[c]) + (north[c] + south[c]))
                for c in range(FIELDS)
            ]
            spread = courant * ((east[0] - west[0]) + (north[1] - south[1]))
            push_x = courant * ((east[3] - west[3]) + (east[2] - west[2]))
            push_y = courant * ((north[3] - south[3]) + (north[2] - south[2]))
            out = [base[0] - push_x, base[1] - push_y, base[2] - 0.25 * spread, base[3] - spread]
            for c in range(FIELDS):
                target[group, at + k, c, :, pl.ds(j * LANES, LANES)] = out[c]
        mid, down_before = mid_next, down
        up, down = up_next, down_next


def quarter(code):
    cosine = jnp.where(code == 0, 1.0, jnp.where(code == 2, -1.0, 0.0))
    sine = jnp.where(code == 1, 1.0, jnp.where(code == 3, -1.0, 0.0))
    return cosine.astype(f32), sine.astype(f32)


def per_level(scalars, group):
    level = lax.broadcasted_iota(jnp.int32, (GROUP, LANES), 0)
    out = jnp.zeros((GROUP, LANES), f32)
    for k in range(GROUP):
        out = jnp.where(level == k, scalars[group * GROUP + k], out)
    return out


def split(value):
    high = value.astype(bf16)
    return high, (value - high.astype(f32)).astype(bf16)


def kernel(
    n_face, n_tile, cols, halo,
    wave_in, turns_in, mass_in, counts_in, state, source, row, weight,
    fields_out, means_out,
    first, odd, even, slab, cells, picked, courants, masses, rows, weights,
    spots0, spots1, sums, inbox, wave, turns, mass, counts,
    load_sem, row_sem, weight_sem, scalar_sem, store_sem, spot_sem, send_sem, recv_sem,
    out_sem, in_sem, meet,
):
    face, tile = lax.axis_index("face"), lax.axis_index("tile")
    devices = n_face * n_tile
    me = face * n_tile + tile
    levels = wave.shape[0]
    groups = levels // GROUP
    width = state.shape[2]
    repeat = width // LANES
    mesh_id = pl.DeviceIdType.MESH

    def place(index):
        index = lax.rem(index, devices)
        return lax.div(index, n_tile), lax.rem(index, n_tile)

    right, left = place(me + 1), place(me + devices - 1)

    def lanes_of(ref, j):
        return ref.at[:, :, pl.ds(j * LANES, LANES)]

    def load(g, j):
        half = pl.ds(g * GROUP * cols, GROUP * cols)
        return pltpu.make_async_copy(
            state.at[:, half, pl.ds(j * LANES, LANES)], slab.at[:, j, half], load_sem.at[g, j]
        )

    for g in range(groups):
        for j in range(repeat):
            load(g, j).start()
    row_load = pltpu.make_async_copy(row, rows, row_sem)
    row_load.start()
    weight_load = pltpu.make_async_copy(weight, weights, weight_sem)
    weight_load.start()

    scalars = [(wave_in, wave), (turns_in, turns), (mass_in, mass), (counts_in, counts)]
    scalar_loads = [
        pltpu.make_async_copy(there, here, scalar_sem.at[k])
        for k, (there, here) in enumerate(scalars)
    ]
    for scalar_load in scalar_loads:
        scalar_load.start()

    barrier = pltpu.get_barrier_semaphore()

    def partner(b):
        bit = lax.rem(lax.div(me, 1 << b), 2)
        return place(me + (1 - 2 * bit) * (1 << b))

    partners = devices.bit_length() - 1
    greeted = [right, left] + [partner(b) for b in range(partners)]
    for device in greeted:
        pl.semaphore_signal(barrier, inc=1, device_id=device, device_id_type=mesh_id)

    def tell(b):
        pl.semaphore_signal(meet.at[b], inc=1, device_id=partner(b), device_id_type=mesh_id)

    def hear(b):
        pl.semaphore_wait(meet.at[b], 1)

    for scalar_load in scalar_loads:
        scalar_load.wait()
    for g in range(groups):
        courants[g] = 5.0 * per_level(wave, g)
        masses[g] = per_level(mass, g)

    def wide(value):
        return jnp.concatenate([value] * repeat, axis=1)

    def lift(g, x):
        for c in range(FIELDS):
            for j in range(repeat):
                lifted = slab[c, j, pl.ds(g * GROUP * cols + x, GROUP, stride=cols), :]
                lifted = 0.5 * lifted if c == 2 else lifted
                first[g, x + halo, c, :, pl.ds(j * LANES, LANES)] = lifted

    def lift_edges(g):
        for j in range(repeat):
            load(g, j).wait()

        def lift_edge(i, carry):
            lift(g, i + (cols - 2 * halo) * lax.div(i, halo))
            return carry

        lax.fori_loop(0, 2 * halo, lift_edge, 0)

    lift_edges(0)
    pl.semaphore_wait(barrier, len(greeted))

    messages = [(g, 1, halo) for g in range(groups - 1)]
    messages += [(groups - 1, k, 1) for k in range(1, halo + 1)]

    def halo_copy(side, m):
        g, k, count = messages[m]
        far = k + count - 1
        if side == 0:
            here, there, to = cols + halo - far, halo - far, right
        else:
            here, there, to = halo + k - 1, cols + halo + k - 1, left
        return pltpu.make_async_remote_copy(
            src_ref=first.at[g, pl.ds(here, count)],
            dst_ref=first.at[g, pl.ds(there, count)],
            send_sem=send_sem.at[side, m],
            recv_sem=recv_sem.at[side, m],
            device_id=to,
            device_id_type=mesh_id,
        )

    for m in range(len(messages)):
        g = messages[m][0]
        if m > 0 and g != messages[m - 1][0]:
            lift_edges(g)
        for side in range(2):
            halo_copy(side, m).start()
    tell(0)
    met = 0

    spots = (spots0, spots1)
    rounds = devices // GATHERED
    slots = rows.shape[1]

    def first_band(turn):
        return pl.multiple_of(lax.rem(lax.div(me, GATHERED) + 1 + turn, rounds) * GATHERED, GATHERED)

    def spot_copy(turn, slot):
        return pltpu.make_async_copy(
            source.at[pl.ds(first_band(turn), GATHERED)], spots[slot], spot_sem.at[slot]
        )

    def lift_inner(i, carry):
        n = cols - 2 * halo
        lift(lax.div(i, n), halo + lax.rem(i, n))
        return carry

    lax.fori_loop(0, groups * (cols - 2 * halo), lift_inner, 0)
    spot_copy(0, 0).start()
    spot_copy(1, 1).start()

    steps = [(first, odd), (odd, even), (even, odd), (odd, even)]

    for s, (old, new) in enumerate(steps, 1):

        def inner(g, carry, old=old, new=new, s=s):
            for x in range(s, cols - s, 2):
                strip(old, new, g, x + halo, 2, courants[g])
            return carry

        lax.fori_loop(0, groups, inner, 0)
        if met + 1 < partners:
            hear(met)
            met += 1
            tell(met)

    def finish(x):
        values = {}
        for g in range(groups):
            for c in range(FIELDS):
                value = even[g, x + halo, c] * (2.0 * SCALE if c == 2 else SCALE)
                for j in range(repeat):
                    part = value[:, j * LANES : (j + 1) * LANES]
                    slab[c, j, pl.ds(g * GROUP * cols + x, GROUP, stride=cols), :] = part
                values[c, g] = value
        blocks = [values[c, g] for c in range(FIELDS) for g in range(groups)]
        blocks += [values[1, g] * (wide(masses[g]) + values[3, g]) for g in range(groups)]
        blocks.append(jnp.ones((GROUP, width), f32))
        spare = LANES - GROUP * len(blocks)
        blocks.append(jnp.zeros((spare, width), f32))
        start = pl.multiple_of(x * width, width)
        cells[pl.ds(start, width), :] = jnp.concatenate(blocks, axis=0).T

    def finish_inner(i, carry):
        finish(halo + i)
        return carry

    lax.fori_loop(0, cols - 2 * halo, finish_inner, 0)

    while met + 1 < partners:
        hear(met)
        met += 1
        tell(met)

    west_cos, west_sin = quarter(jnp.where(tile == 0, turns[face], 0))
    east_cos, east_sin = quarter(jnp.where(tile == n_tile - 1, turns[lax.rem(face + 1, n_face)], 0))

    west_turn, east_turn = (west_cos, west_sin), (east_cos, east_sin)
    for m, (g, k, count) in enumerate(messages):
        halo_copy(0, m).wait_recv()
        halo_copy(1, m).wait_recv()
        if count == halo:
            for s, (old, new) in enumerate(steps, 1):
                strip(old, new, g, s, halo, courants[g], {halo - 1 - s: west_turn})
                strip(old, new, g, cols - s + halo, halo, courants[g], {s - 1: east_turn})
            continue
        for s, (old, new) in enumerate(steps, 1):
            x = s - k
            strip(old, new, g, x + halo, 1, courants[g], {-1 - x: west_turn})
            x = cols - 1 + k - s
            strip(old, new, g, x + halo, 1, courants[g], {cols - 1 - x: east_turn})
        finish(halo - k)
        finish(cols - 1 - halo + k)

    stores = [
        pltpu.make_async_copy(slab.at[:, j], lanes_of(fields_out, j), store_sem.at[j])
        for j in range(repeat)
    ]
    for store in stores:
        store.start()

    row_load.wait()
    weight_load.wait()
    hear(met)
    def pick(slot):
        for k in range(GATHERED):
            for j in range(slots):
                picked[slot, k, pl.ds(j, 1), :] = cells[pl.ds(spots[slot][k, j], 1), :]

    sub = lax.broadcasted_iota(jnp.int32, (2 * BAND_ROWS, slots), 0)
    link = lax.broadcasted_iota(jnp.int32, (2 * BAND_ROWS, slots), 1)

    def add_up(turn, slot):
        start = first_band(turn)
        for k in range(GATHERED):
            band = start + k
            w = weights[pl.ds(band, 1), :]
            high = w.astype(bf16).astype(f32)
            part = jnp.where(sub < BAND_ROWS, high, w - high)
            mine = (rows[pl.ds(band, 1), :] == lax.rem(sub, BAND_ROWS)) & (link < counts[band])
            lhs = jnp.where(mine, part, 0.0).astype(bf16)
            high_cells, low_cells = split(picked[slot, k])
            product = jnp.dot(
                lhs,
                jnp.concatenate([high_cells, low_cells], axis=1),
                preferred_element_type=f32,
            )
            sums[band] = (
                product[:BAND_ROWS, :LANES]
                + product[:BAND_ROWS, LANES:]
                + product[BAND_ROWS:, :LANES]
            )

    def send_band(band):
        pltpu.make_async_remote_copy(
            src_ref=sums.at[band],
            dst_ref=inbox.at[me],
            send_sem=out_sem,
            recv_sem=in_sem,
            device_id=place(band),
            device_id_type=mesh_id,
        ).start()

    def send(turn):
        for k in range(GATHERED):
            send_band(first_band(turn) + k)

    def send_last():
        for k in range(1, GATHERED):
            send_band(first_band(rounds - 1) + lax.rem(me + k, GATHERED))
        inbox[me] = sums[me]

    spot_copy(0, 0).wait()
    pick(0)
    spot_copy(2, 0).start()

    def two_rounds(i, carry):
        for slot in (1, 0):
            turn = 2 * i + 2 - slot
            spot_copy(turn, slot).wait()
            pick(slot)
            add_up(turn - 1, 1 - slot)
            spot_copy(turn + 2, slot).start()
            send(turn - 1)
        return carry

    lax.fori_loop(0, rounds // 2 - 1, two_rounds, 0)
    spot_copy(rounds - 1, 1).wait()
    spot_copy(rounds, 0).wait()
    pick(1)
    add_up(rounds - 2, 0)
    send(rounds - 2)
    add_up(rounds - 1, 1)
    send_last()

    others = pltpu.make_async_remote_copy(
        src_ref=sums.at[pl.ds(0, devices - 1)],
        dst_ref=inbox.at[pl.ds(0, devices - 1)],
        send_sem=out_sem,
        recv_sem=in_sem,
        device_id=right,
        device_id_type=mesh_id,
    )
    lat_row = me * BAND_ROWS + lax.broadcasted_iota(jnp.int32, (BAND_ROWS, LANES), 0)
    total_rows = BAND_ROWS * devices
    phi = ((lat_row.astype(f32) + 0.5) / total_rows - 0.5) * (jnp.pi / 2)
    cosine = jnp.cos(phi)
    others.wait_recv()
    total = jnp.sum(inbox[...], axis=0)
    ones_at = (FIELDS + 1) * levels
    means = total / jnp.broadcast_to(total[:, ones_at : ones_at + 1], total.shape)
    zonal = means
    lane = lax.broadcasted_iota(jnp.int32, means.shape, 1)
    k = 1
    while k < levels:
        means = means + jnp.where(lane >= FIELDS * levels + k, pltpu.roll(means, k, 1), 0.0)
        k *= 2
    stream = cosine * means
    means_out[...] = jnp.where(lane < FIELDS * levels, zonal, stream)

    for m in range(len(messages)):
        for side in range(2):
            halo_copy(side, m).wait_send()
    others.wait_send()
    for store in stores:
        store.wait()


def hand_over(
    fields_in, means_in, new_state, zonal_out, stream_out,
    held, means, zonal, stream, in_sem, out_sem, small_sem,
):
    parts, length = held.shape[0], held.shape[2]
    per_field = parts // FIELDS

    def piece(ref, k):
        return ref.at[k // per_field, pl.ds(k % per_field * length, length)]

    loads = [
        pltpu.make_async_copy(piece(fields_in, k), held.at[k, 0], in_sem.at[k])
        for k in range(parts)
    ]
    stores = [
        pltpu.make_async_copy(held.at[k, 0], piece(new_state, k), out_sem.at[k])
        for k in range(parts)
    ]
    load_means = pltpu.make_async_copy(means_in, means, small_sem.at[0])
    store_zonal = pltpu.make_async_copy(zonal, zonal_out, small_sem.at[1])
    store_stream = pltpu.make_async_copy(stream, stream_out, small_sem.at[2])
    load_means.start()
    for load in loads:
        load.start()
    load_means.wait()
    count = zonal.shape[1]
    zonal[...] = means[:, :count]
    stream[...] = means[:, count : count + stream.shape[1]]
    store_zonal.start()
    store_stream.start()
    for load, store in zip(loads, stores):
        load.wait()
        store.start()
    for store in [store_zonal, store_stream, *stores]:
        store.wait()


def on_device(n_face, n_tile, state, wave, turns, mass, source, row, weight, count):
    fields, levels, cols, width = state.shape
    halo = SUBSTEPS
    groups = levels // GROUP
    devices = n_face * n_tile
    slots = source.shape[2]
    merged = (fields, levels * cols, width)
    vmem = pl.BlockSpec(memory_space=pltpu.VMEM)
    hbm = pl.BlockSpec(memory_space=pltpu.HBM)
    field = pltpu.VMEM((groups, cols + 2 * halo, fields, GROUP, width), f32)
    dma = pltpu.SemaphoreType.DMA

    def body(*refs):
        kernel(n_face, n_tile, cols, halo, *refs)

    new_fields, means = pl.pallas_call(
        body,
        out_shape=(
            jax.ShapeDtypeStruct(merged, f32),
            jax.ShapeDtypeStruct((BAND_ROWS, LANES), f32),
        ),
        in_specs=[hbm] * 8,
        out_specs=(hbm, vmem),
        scratch_shapes=[
            field,
            field,
            field,
            pltpu.VMEM((fields, width // LANES, levels * cols, LANES), f32),
            pltpu.VMEM((cols * width, LANES), f32),
            pltpu.VMEM((2, GATHERED, slots, LANES), f32),
            pltpu.VMEM((groups, GROUP, LANES), f32),
            pltpu.VMEM((groups, GROUP, LANES), f32),
            pltpu.VMEM((devices, slots), jnp.int32),
            pltpu.VMEM((devices, slots), f32),
            pltpu.SMEM((GATHERED, slots), jnp.int32),
            pltpu.SMEM((GATHERED, slots), jnp.int32),
            pltpu.VMEM((devices, BAND_ROWS, LANES), f32),
            pltpu.VMEM((devices, BAND_ROWS, LANES), f32),
            pltpu.SMEM((levels,), f32),
            pltpu.SMEM((n_face,), jnp.int32),
            pltpu.SMEM((levels,), f32),
            pltpu.SMEM((devices,), jnp.int32),
            dma((groups, width // LANES)),
            dma,
            dma,
            dma((4,)),
            dma((width // LANES,)),
            dma((2,)),
            dma((2, groups - 1 + halo)),
            dma((2, groups - 1 + halo)),
            dma,
            dma,
            pltpu.SemaphoreType.REGULAR((devices.bit_length() - 1,)),
        ],
        compiler_params=pltpu.CompilerParams(
            collective_id=1, has_side_effects=True, vmem_limit_bytes=57 * 2**20
        ),
    )(
        wave,
        turns,
        mass,
        count[0],
        state.reshape(merged),
        source[0],
        row[0],
        weight[0],
    )
    new_state, zonal, stream = pl.pallas_call(
        hand_over,
        out_shape=(
            jax.ShapeDtypeStruct(merged, f32),
            jax.ShapeDtypeStruct((BAND_ROWS, fields * levels), f32),
            jax.ShapeDtypeStruct((BAND_ROWS, levels), f32),
        ),
        in_specs=[hbm, hbm],
        out_specs=(hbm, hbm, hbm),
        scratch_shapes=[
            pltpu.VMEM((HANDED, 1, fields * levels * cols // HANDED, width), f32),
            pltpu.VMEM((BAND_ROWS, LANES), f32),
            pltpu.VMEM((BAND_ROWS, fields * levels), f32),
            pltpu.VMEM((BAND_ROWS, levels), f32),
            dma((HANDED,)),
            dma((HANDED,)),
            dma((3,)),
        ],
        compiler_params=pltpu.CompilerParams(vmem_limit_bytes=57 * 2**20),
    )(new_fields, means)
    return new_state.reshape(state.shape), zonal, stream


def solution(mesh):
    n_face, n_tile = mesh.shape["face"], mesh.shape["tile"]
    both = ("face", "tile")
    zonal_dim = P(None, None, both, None)
    links = P(both, None, None)

    def program(*args):
        return on_device(n_face, n_tile, *args)

    return jax.shard_map(
        program,
        mesh=mesh,
        in_specs=(zonal_dim, P(), P(), P(), links, links, links, P(both, None)),
        out_specs=(zonal_dim, P(both, None), P(both, None)),
        check_vma=False,
    )
```

```python
import jax
import jax.numpy as jnp
from jax import lax
from jax.experimental import pallas as pl
from jax.experimental.pallas import tpu as pltpu
from jax.sharding import PartitionSpec as P

SUBSTEPS = 4
BAND_ROWS = 4
FIELDS = 4
GROUP = 8
LANES = 128
GATHERED = 8
HANDED = 4
SCALE = 10.0**-SUBSTEPS

f32 = jnp.float32
bf16 = jnp.bfloat16


def turned(wind, turn):
    cosine, sine = turn
    east, north = wind
    return cosine * east - sine * north, sine * east + cosine * north


def strip(source, target, group, at, count, courant, turns=None):
    turns = turns or {}
    blocks = source.shape[4] // LANES
    lane = lax.broadcasted_iota(jnp.int32, (GROUP, LANES), 1)
    first_lane, last_lane = lane == 0, lane == LANES - 1
    inside = range(count)

    def mids(j):
        return {
            (k, c): source[group, at + k, c, :, pl.ds(j * LANES, LANES)]
            for k in inside
            for c in range(FIELDS)
        }

    def rolls(mid, amount):
        return {key: pltpu.roll(q, amount, 1) for key, q in mid.items()}

    mid = mids(0)
    up, down = rolls(mid, LANES - 1), rolls(mid, 1)
    zeros = {key: jnp.zeros((GROUP, LANES), f32) for key in mid}
    down_before = zeros
    for j in range(blocks):
        if j + 1 < blocks:
            mid_next = mids(j + 1)
            up_next, down_next = rolls(mid_next, LANES - 1), rolls(mid_next, 1)
        else:
            mid_next, up_next, down_next = None, zeros, None
        here = dict(mid)
        for k in (-1, count):
            for c in range(FIELDS):
                here[k, c] = source[group, at + k, c, :, pl.ds(j * LANES, LANES)]
        for k in inside:
            west = [here[k - 1, c] for c in range(FIELDS)]
            east = [here[k + 1, c] for c in range(FIELDS)]
            if k - 1 in turns:
                west[:2] = turned(west[:2], turns[k - 1])
            if k in turns:
                cosine, sine = turns[k]
                east[:2] = turned(east[:2], (cosine, -sine))
            north = [jnp.where(last_lane, up_next[k, c], up[k, c]) for c in range(FIELDS)]
            south = [jnp.where(first_lane, down_before[k, c], down[k, c]) for c in range(FIELDS)]
            base = [
                6.0 * mid[k, c] + ((west[c] + east[c]) + (north[c] + south[c]))
                for c in range(FIELDS)
            ]
            spread = courant * ((east[0] - west[0]) + (north[1] - south[1]))
            push_x = courant * ((east[3] - west[3]) + (east[2] - west[2]))
            push_y = courant * ((north[3] - south[3]) + (north[2] - south[2]))
            out = [base[0] - push_x, base[1] - push_y, base[2] - 0.25 * spread, base[3] - spread]
            for c in range(FIELDS):
                target[group, at + k, c, :, pl.ds(j * LANES, LANES)] = out[c]
        mid, down_before = mid_next, down
        up, down = up_next, down_next


def quarter(code):
    cosine = jnp.where(code == 0, 1.0, jnp.where(code == 2, -1.0, 0.0))
    sine = jnp.where(code == 1, 1.0, jnp.where(code == 3, -1.0, 0.0))
    return cosine.astype(f32), sine.astype(f32)


def per_level(scalars, group):
    level = lax.broadcasted_iota(jnp.int32, (GROUP, LANES), 0)
    out = jnp.zeros((GROUP, LANES), f32)
    for k in range(GROUP):
        out = jnp.where(level == k, scalars[group * GROUP + k], out)
    return out


def split(value):
    high = value.astype(bf16)
    return high, (value - high.astype(f32)).astype(bf16)


def kernel(
    n_face, n_tile, cols, halo,
    wave_in, turns_in, mass_in, counts_in, state, source, row, weight,
    fields_out, means_out,
    first, odd, even, slab, cells, picked, courants, masses, rows, weights,
    spots0, spots1, sums, inbox, wave, turns, mass, counts,
    load_sem, row_sem, weight_sem, scalar_sem, store_sem, spot_sem, send_sem, recv_sem,
    out_sem, in_sem, meet,
):
    face, tile = lax.axis_index("face"), lax.axis_index("tile")
    devices = n_face * n_tile
    me = face * n_tile + tile
    levels = wave.shape[0]
    groups = levels // GROUP
    width = state.shape[2]
    repeat = width // LANES
    mesh_id = pl.DeviceIdType.MESH

    def place(index):
        index = lax.rem(index, devices)
        return lax.div(index, n_tile), lax.rem(index, n_tile)

    right, left = place(me + 1), place(me + devices - 1)

    def lanes_of(ref, j):
        return ref.at[:, :, pl.ds(j * LANES, LANES)]

    def load(g, j):
        half = pl.ds(g * GROUP * cols, GROUP * cols)
        return pltpu.make_async_copy(
            state.at[:, half, pl.ds(j * LANES, LANES)], slab.at[:, j, half], load_sem.at[g, j]
        )

    for g in range(groups):
        for j in range(repeat):
            load(g, j).start()
    row_load = pltpu.make_async_copy(row, rows, row_sem)
    row_load.start()
    weight_load = pltpu.make_async_copy(weight, weights, weight_sem)
    weight_load.start()

    scalars = [(wave_in, wave), (turns_in, turns), (mass_in, mass), (counts_in, counts)]
    scalar_loads = [
        pltpu.make_async_copy(there, here, scalar_sem.at[k])
        for k, (there, here) in enumerate(scalars)
    ]
    for scalar_load in scalar_loads:
        scalar_load.start()

    barrier = pltpu.get_barrier_semaphore()

    def partner(b):
        bit = lax.rem(lax.div(me, 1 << b), 2)
        return place(me + (1 - 2 * bit) * (1 << b))

    partners = devices.bit_length() - 1
    greeted = [right, left] + [partner(b) for b in range(partners)]
    for device in greeted:
        pl.semaphore_signal(barrier, inc=1, device_id=device, device_id_type=mesh_id)

    def tell(b):
        pl.semaphore_signal(meet.at[b], inc=1, device_id=partner(b), device_id_type=mesh_id)

    def hear(b):
        pl.semaphore_wait(meet.at[b], 1)

    for scalar_load in scalar_loads:
        scalar_load.wait()
    for g in range(groups):
        courants[g] = 5.0 * per_level(wave, g)
        masses[g] = per_level(mass, g)

    def wide(value):
        return jnp.concatenate([value] * repeat, axis=1)

    def lift(g, x):
        for c in range(FIELDS):
            for j in range(repeat):
                lifted = slab[c, j, pl.ds(g * GROUP * cols + x, GROUP, stride=cols), :]
                lifted = 0.5 * lifted if c == 2 else lifted
                first[g, x + halo, c, :, pl.ds(j * LANES, LANES)] = lifted

    def lift_edges(g):
        for j in range(repeat):
            load(g, j).wait()

        def lift_edge(i, carry):
            lift(g, i + (cols - 2 * halo) * lax.div(i, halo))
            return carry

        lax.fori_loop(0, 2 * halo, lift_edge, 0)

    lift_edges(0)
    pl.semaphore_wait(barrier, len(greeted))

    messages = [(g, 1, halo) for g in range(groups - 1)]
    messages += [(groups - 1, k, 1) for k in range(1, halo + 1)]

    def halo_copy(side, m):
        g, k, count = messages[m]
        far = k + count - 1
        if side == 0:
            here, there, to = cols + halo - far, halo - far, right
        else:
            here, there, to = halo + k - 1, cols + halo + k - 1, left
        return pltpu.make_async_remote_copy(
            src_ref=first.at[g, pl.ds(here, count)],
            dst_ref=first.at[g, pl.ds(there, count)],
            send_sem=send_sem.at[side, m],
            recv_sem=recv_sem.at[side, m],
            device_id=to,
            device_id_type=mesh_id,
        )

    for m in range(len(messages)):
        g = messages[m][0]
        if m > 0 and g != messages[m - 1][0]:
            lift_edges(g)
        for side in range(2):
            halo_copy(side, m).start()
    tell(0)
    met = 0

    spots = (spots0, spots1)
    rounds = devices // GATHERED
    slots = rows.shape[1]

    def first_band(turn):
        return pl.multiple_of(lax.rem(lax.div(me, GATHERED) + 1 + turn, rounds) * GATHERED, GATHERED)

    def spot_copy(turn, slot):
        return pltpu.make_async_copy(
            source.at[pl.ds(first_band(turn), GATHERED)], spots[slot], spot_sem.at[slot]
        )

    def lift_inner(i, carry):
        n = cols - 2 * halo
        lift(lax.div(i, n), halo + lax.rem(i, n))
        return carry

    lax.fori_loop(0, groups * (cols - 2 * halo), lift_inner, 0)
    spot_copy(0, 0).start()
    spot_copy(1, 1).start()

    steps = [(first, odd), (odd, even), (even, odd), (odd, even)]

    for s, (old, new) in enumerate(steps, 1):

        def inner(g, carry, old=old, new=new, s=s):
            for x in range(s, cols - s, 2):
                strip(old, new, g, x + halo, 2, courants[g])
            return carry

        lax.fori_loop(0, groups, inner, 0)
        if met + 1 < partners:
            hear(met)
            met += 1
            tell(met)

    def finish(x):
        values = {}
        for g in range(groups):
            for c in range(FIELDS):
                value = even[g, x + halo, c] * (2.0 * SCALE if c == 2 else SCALE)
                for j in range(repeat):
                    part = value[:, j * LANES : (j + 1) * LANES]
                    slab[c, j, pl.ds(g * GROUP * cols + x, GROUP, stride=cols), :] = part
                values[c, g] = value
        blocks = [values[c, g] for c in range(FIELDS) for g in range(groups)]
        blocks += [values[1, g] * (wide(masses[g]) + values[3, g]) for g in range(groups)]
        blocks.append(jnp.ones((GROUP, width), f32))
        spare = LANES - GROUP * len(blocks)
        blocks.append(jnp.zeros((spare, width), f32))
        start = pl.multiple_of(x * width, width)
        cells[pl.ds(start, width), :] = jnp.concatenate(blocks, axis=0).T

    def finish_inner(i, carry):
        finish(halo + i)
        return carry

    lax.fori_loop(0, cols - 2 * halo, finish_inner, 0)

    while met + 1 < partners:
        hear(met)
        met += 1
        tell(met)

    west_cos, west_sin = quarter(jnp.where(tile == 0, turns[face], 0))
    east_cos, east_sin = quarter(jnp.where(tile == n_tile - 1, turns[lax.rem(face + 1, n_face)], 0))

    west_turn, east_turn = (west_cos, west_sin), (east_cos, east_sin)
    for m, (g, k, count) in enumerate(messages):
        halo_copy(0, m).wait_recv()
        halo_copy(1, m).wait_recv()
        if count == halo:
            for s, (old, new) in enumerate(steps, 1):
                strip(old, new, g, s, halo, courants[g], {halo - 1 - s: west_turn})
                strip(old, new, g, cols - s + halo, halo, courants[g], {s - 1: east_turn})
            continue
        for s, (old, new) in enumerate(steps, 1):
            x = s - k
            strip(old, new, g, x + halo, 1, courants[g], {-1 - x: west_turn})
            x = cols - 1 + k - s
            strip(old, new, g, x + halo, 1, courants[g], {cols - 1 - x: east_turn})
        finish(halo - k)
        finish(cols - 1 - halo + k)

    stores = [
        pltpu.make_async_copy(slab.at[:, j], lanes_of(fields_out, j), store_sem.at[j])
        for j in range(repeat)
    ]
    for store in stores:
        store.start()

    row_load.wait()
    weight_load.wait()
    hear(met)
    def pick(slot):
        for k in range(GATHERED):
            for j in range(slots):
                picked[slot, k, pl.ds(j, 1), :] = cells[pl.ds(spots[slot][k, j], 1), :]

    sub = lax.broadcasted_iota(jnp.int32, (2 * BAND_ROWS, slots), 0)
    link = lax.broadcasted_iota(jnp.int32, (2 * BAND_ROWS, slots), 1)

    def add_up(turn, slot):
        start = first_band(turn)
        for k in range(GATHERED):
            band = start + k
            w = weights[pl.ds(band, 1), :]
            high = w.astype(bf16).astype(f32)
            part = jnp.where(sub < BAND_ROWS, high, w - high)
            mine = (rows[pl.ds(band, 1), :] == lax.rem(sub, BAND_ROWS)) & (link < counts[band])
            lhs = jnp.where(mine, part, 0.0).astype(bf16)
            high_cells, low_cells = split(picked[slot, k])
            product = jnp.dot(
                lhs,
                jnp.concatenate([high_cells, low_cells], axis=1),
                preferred_element_type=f32,
            )
            sums[band] = (
                product[:BAND_ROWS, :LANES]
                + product[:BAND_ROWS, LANES:]
                + product[BAND_ROWS:, :LANES]
            )

    def send_band(band):
        pltpu.make_async_remote_copy(
            src_ref=sums.at[band],
            dst_ref=inbox.at[me],
            send_sem=out_sem,
            recv_sem=in_sem,
            device_id=place(band),
            device_id_type=mesh_id,
        ).start()

    def send(turn):
        for k in range(GATHERED):
            send_band(first_band(turn) + k)

    def send_last():
        for k in range(1, GATHERED):
            send_band(first_band(rounds - 1) + lax.rem(me + k, GATHERED))
        inbox[me] = sums[me]

    spot_copy(0, 0).wait()
    pick(0)
    spot_copy(2, 0).start()

    def two_rounds(i, carry):
        for slot in (1, 0):
            turn = 2 * i + 2 - slot
            spot_copy(turn, slot).wait()
            pick(slot)
            add_up(turn - 1, 1 - slot)
            spot_copy(turn + 2, slot).start()
            send(turn - 1)
        return carry

    lax.fori_loop(0, rounds // 2 - 1, two_rounds, 0)
    spot_copy(rounds - 1, 1).wait()
    spot_copy(rounds, 0).wait()
    pick(1)
    add_up(rounds - 2, 0)
    send(rounds - 2)
    add_up(rounds - 1, 1)
    send_last()

    others = pltpu.make_async_remote_copy(
        src_ref=sums.at[pl.ds(0, devices - 1)],
        dst_ref=inbox.at[pl.ds(0, devices - 1)],
        send_sem=out_sem,
        recv_sem=in_sem,
        device_id=right,
        device_id_type=mesh_id,
    )
    lat_row = me * BAND_ROWS + lax.broadcasted_iota(jnp.int32, (BAND_ROWS, LANES), 0)
    total_rows = BAND_ROWS * devices
    phi = ((lat_row.astype(f32) + 0.5) / total_rows - 0.5) * (jnp.pi / 2)
    cosine = jnp.cos(phi)
    for m in range(len(messages)):
        for side in range(2):
            halo_copy(side, m).wait_send()
    others.wait_send()
    for store in stores:
        store.wait()
    others.wait_recv()
    chains = inbox[...].reshape(devices // GATHERED, GATHERED, BAND_ROWS, LANES)
    total = jnp.sum(jnp.sum(chains, axis=0), axis=0)
    ones_at = (FIELDS + 1) * levels
    means = total / jnp.broadcast_to(total[:, ones_at : ones_at + 1], total.shape)
    zonal = means
    lane = lax.broadcasted_iota(jnp.int32, means.shape, 1)
    k = 1
    while k < levels:
        means = means + jnp.where(lane >= FIELDS * levels + k, pltpu.roll(means, k, 1), 0.0)
        k *= 2
    stream = cosine * means
    means_out[...] = jnp.where(lane < FIELDS * levels, zonal, stream)


def hand_over(
    fields_in, means_in, new_state, zonal_out, stream_out,
    held, means, zonal, stream, in_sem, out_sem, small_sem,
):
    parts, length = held.shape[0], held.shape[2]
    per_field = parts // FIELDS

    def piece(ref, k):
        return ref.at[k // per_field, pl.ds(k % per_field * length, length)]

    loads = [
        pltpu.make_async_copy(piece(fields_in, k), held.at[k, 0], in_sem.at[k])
        for k in range(parts)
    ]
    stores = [
        pltpu.make_async_copy(held.at[k, 0], piece(new_state, k), out_sem.at[k])
        for k in range(parts)
    ]
    load_means = pltpu.make_async_copy(means_in, means, small_sem.at[0])
    store_zonal = pltpu.make_async_copy(zonal, zonal_out, small_sem.at[1])
    store_stream = pltpu.make_async_copy(stream, stream_out, small_sem.at[2])
    load_means.start()
    for load in loads:
        load.start()
    load_means.wait()
    count = zonal.shape[1]
    zonal[...] = means[:, :count]
    stream[...] = means[:, count : count + stream.shape[1]]
    store_zonal.start()
    store_stream.start()
    for load, store in zip(loads, stores):
        load.wait()
        store.start()
    for store in [store_zonal, store_stream, *stores]:
        store.wait()


def on_device(n_face, n_tile, state, wave, turns, mass, source, row, weight, count):
    fields, levels, cols, width = state.shape
    halo = SUBSTEPS
    groups = levels // GROUP
    devices = n_face * n_tile
    slots = source.shape[2]
    merged = (fields, levels * cols, width)
    vmem = pl.BlockSpec(memory_space=pltpu.VMEM)
    hbm = pl.BlockSpec(memory_space=pltpu.HBM)
    field = pltpu.VMEM((groups, cols + 2 * halo, fields, GROUP, width), f32)
    dma = pltpu.SemaphoreType.DMA

    def body(*refs):
        kernel(n_face, n_tile, cols, halo, *refs)

    new_fields, means = pl.pallas_call(
        body,
        out_shape=(
            jax.ShapeDtypeStruct(merged, f32),
            jax.ShapeDtypeStruct((BAND_ROWS, LANES), f32),
        ),
        in_specs=[hbm] * 8,
        out_specs=(hbm, vmem),
        scratch_shapes=[
            field,
            field,
            field,
            pltpu.VMEM((fields, width // LANES, levels * cols, LANES), f32),
            pltpu.VMEM((cols * width, LANES), f32),
            pltpu.VMEM((2, GATHERED, slots, LANES), f32),
            pltpu.VMEM((groups, GROUP, LANES), f32),
            pltpu.VMEM((groups, GROUP, LANES), f32),
            pltpu.VMEM((devices, slots), jnp.int32),
            pltpu.VMEM((devices, slots), f32),
            pltpu.SMEM((GATHERED, slots), jnp.int32),
            pltpu.SMEM((GATHERED, slots), jnp.int32),
            pltpu.VMEM((devices, BAND_ROWS, LANES), f32),
            pltpu.VMEM((devices, BAND_ROWS, LANES), f32),
            pltpu.SMEM((levels,), f32),
            pltpu.SMEM((n_face,), jnp.int32),
            pltpu.SMEM((levels,), f32),
            pltpu.SMEM((devices,), jnp.int32),
            dma((groups, width // LANES)),
            dma,
            dma,
            dma((4,)),
            dma((width // LANES,)),
            dma((2,)),
            dma((2, groups - 1 + halo)),
            dma((2, groups - 1 + halo)),
            dma,
            dma,
            pltpu.SemaphoreType.REGULAR((devices.bit_length() - 1,)),
        ],
        compiler_params=pltpu.CompilerParams(
            collective_id=1, has_side_effects=True, vmem_limit_bytes=57 * 2**20
        ),
    )(
        wave,
        turns,
        mass,
        count[0],
        state.reshape(merged),
        source[0],
        row[0],
        weight[0],
    )
    new_state, zonal, stream = pl.pallas_call(
        hand_over,
        out_shape=(
            jax.ShapeDtypeStruct(merged, f32),
            jax.ShapeDtypeStruct((BAND_ROWS, fields * levels), f32),
            jax.ShapeDtypeStruct((BAND_ROWS, levels), f32),
        ),
        in_specs=[hbm, hbm],
        out_specs=(hbm, hbm, hbm),
        scratch_shapes=[
            pltpu.VMEM((HANDED, 1, fields * levels * cols // HANDED, width), f32),
            pltpu.VMEM((BAND_ROWS, LANES), f32),
            pltpu.VMEM((BAND_ROWS, fields * levels), f32),
            pltpu.VMEM((BAND_ROWS, levels), f32),
            dma((HANDED,)),
            dma((HANDED,)),
            dma((3,)),
        ],
        compiler_params=pltpu.CompilerParams(vmem_limit_bytes=57 * 2**20),
    )(new_fields, means)
    return new_state.reshape(state.shape), zonal, stream


def solution(mesh):
    n_face, n_tile = mesh.shape["face"], mesh.shape["tile"]
    both = ("face", "tile")
    zonal_dim = P(None, None, both, None)
    links = P(both, None, None)

    def program(*args):
        return on_device(n_face, n_tile, *args)

    return jax.shard_map(
        program,
        mesh=mesh,
        in_specs=(zonal_dim, P(), P(), P(), links, links, links, P(both, None)),
        out_specs=(zonal_dim, P(both, None), P(both, None)),
        check_vma=False,
    )
```
